256 devices in a mesh: row: 32 (over z_hi, y, x), col: 8 (over z_lo, core).
Axes of the slice: x: 4, y: 4, z: 8 (z_hi: 2, z_lo: 4; z = z_hi * 4 + z_lo), core: 2. Of those that a mesh axis runs over, the one named last changes fastest.
Arguments:
- counts: int32 [8192, 8192], P('row', 'col'), may hold values from 0 to 63
- inverse_capacity: float32 [8192, 8192], P('row', 'col'), may hold values from 0.25 to 2, as said below
Outputs:
- field_first: float32 [8192, 8192], P('row', 'col')
- field_second: float32 [8192, 8192], P('row', 'col')
The draws below stay inside these ranges and needn't reach their ends.
Inputs may be any that keep to these rules, and one draw needn't show every extreme that they name: `inverse_capacity`: positive.
All inputs are finite; a program needn't handle non-finite values.
Results may differ from the reference program's by a relative error of at most 0.002.
Values sent between devices are 32-bit elements; how exact they have to be, the bound alone decides.
A program may use at most 64 MiB of HBM per device.

```python
import math
import jax
import jax.numpy as jnp
from jax import lax

BIN_ROWS = 8192
BIN_COLUMNS = 8192


def draw_inverse_capacity(key, part):
    key = jax.random.fold_in(key, 7)
    roughness = jax.random.uniform(key, (BIN_ROWS, BIN_COLUMNS), jnp.float32, -1.0, 1.0)
    return jnp.exp2(roughness)


def plant(values, rng, low, largest):
    index_at = [jax.random.randint(jax.random.fold_in(rng, axis), (), 0, length) for axis, length in enumerate(values.shape)]
    widest = values.shape.index(max(values.shape))
    next_to = index_at[:widest] + [(index_at[widest] + 1) % values.shape[widest]] + index_at[widest + 1:]
    return values.at[tuple(index_at)].set(low).at[tuple(next_to)].set(largest)


def setup_inputs(seed: int = 0) -> dict:
    streams_of = jax.random.split(jax.random.key(seed), 3)
    counts = plant(jax.random.randint(streams_of[0], (BIN_ROWS, BIN_COLUMNS), 0, 64), jax.random.fold_in(streams_of[0], 1), 0, 63).astype(jnp.int32)
    inverse_capacity = draw_inverse_capacity(jax.random.fold_in(streams_of[2], 71), 0)
    return dict(counts=counts, inverse_capacity=inverse_capacity)


def by_blocks(transform, matrix):
    height = matrix.shape[0]
    pieces = max(1, height // 256)
    shaped = matrix.reshape(pieces, height // pieces, matrix.shape[1])
    return lax.map(transform, shaped).reshape(height, matrix.shape[1])

def phase_table(length):
    return jnp.arange(length, dtype=jnp.int32).astype(jnp.float32) * (math.pi / (2.0 * length))

def cosine_forward(matrix):
    length = matrix.shape[1]
    folded = jnp.concatenate([matrix[:, 0::2], jnp.flip(matrix[:, 1::2], axis=1)], axis=1)
    spectrum = jnp.fft.fft(folded, axis=1)
    phases = phase_table(length)
    return jnp.real(spectrum) * jnp.cos(phases) + jnp.imag(spectrum) * jnp.sin(phases)

def reversed_partner(matrix):
    return jnp.concatenate([jnp.zeros_like(matrix[:, :1]), jnp.flip(matrix[:, 1:], axis=1)], axis=1)

def cosine_sum(matrix):
    length = matrix.shape[1]
    doubled = matrix.at[:, 0].multiply(2.0)
    partner = reversed_partner(matrix)
    phases = phase_table(length)
    real_part = jnp.cos(phases) * doubled + jnp.sin(phases) * partner
    imag_part = jnp.sin(phases) * doubled - jnp.cos(phases) * partner
    folded = jnp.real(jnp.fft.ifft(lax.complex(real_part, imag_part), axis=1)) * (length / 2.0)
    midpoint = length // 2
    even_part = folded[:, :midpoint]
    odd_part = jnp.flip(folded[:, midpoint:], axis=1)
    return jnp.stack([even_part, odd_part], axis=2).reshape(matrix.shape[0], length)

def sine_sum(matrix):
    length = matrix.shape[1]
    parity = 1.0 - 2.0 * (jnp.arange(length, dtype=jnp.int32) % 2).astype(jnp.float32)
    return cosine_sum(reversed_partner(matrix)) * parity[None, :]

def reference(counts, inverse_capacity):
    density = counts.astype(jnp.float32) * inverse_capacity * 0.03125
    along_second = by_blocks(cosine_forward, density)
    norming = 4.0 / math.sqrt(BIN_ROWS * BIN_COLUMNS)
    coefficients = by_blocks(cosine_forward, along_second.T).T * norming
    index_down = jnp.arange(BIN_ROWS, dtype=jnp.int32)
    index_across = jnp.arange(BIN_COLUMNS, dtype=jnp.int32)
    omega_down = math.pi * index_down.astype(jnp.float32)
    omega_across = math.pi * index_across.astype(jnp.float32)
    denominator = omega_down[:, None] * omega_down[:, None] + omega_across[None, :] * omega_across[None, :]
    corner = (index_down[:, None] == 0) & (index_across[None, :] == 0)
    weight = jnp.where(corner, 0.0, 1.0 / jnp.where(corner, 1.0, denominator))
    spectral = coefficients * weight
    first_cosine = by_blocks(cosine_sum, spectral)
    first_sine = by_blocks(sine_sum, spectral * omega_across[None, :])
    field_first = by_blocks(sine_sum, (first_cosine * omega_down[:, None]).T).T
    field_second = by_blocks(cosine_sum, first_sine.T).T
    return (field_first, field_second)
```

```python
import math

import jax
import jax.numpy as jnp
import ml_dtypes
import numpy as np
from jax import lax
from jax.experimental import pallas as pl
from jax.experimental.pallas import tpu as pltpu
from jax.sharding import PartitionSpec as P

MESH = pl.DeviceIdType.MESH
F32 = jnp.float32
BF16 = jnp.bfloat16
ROWS, COLS = 32, 8
DEVICES = ROWS * COLS
LANES = 128
YA, YB = 64, 128
XA, XB = 256, 32
BINS = 8192


def tables(coarse, fine):
    half = fine // 2
    k = np.arange(coarse)[:, None]
    a = np.arange(coarse)[None, :]
    angle = np.pi * (k * a % (2 * coarse)) / coarse
    first = np.concatenate([np.cos(angle), np.sin(angle)], axis=0)
    first[coarse] = 1.0 - 2.0 * (np.arange(coarse) % 2)
    odd = 2 * np.arange(fine)[None, :] + 1
    turn = np.pi * k * odd / (2 * coarse * fine)
    m = np.arange(half)[:, None]
    low = np.pi * (m * odd % (2 * fine)) / fine
    high = np.pi * ((m + 1) * odd % (2 * fine)) / fine
    middle = np.pi * ((2 * m + 1) * odd % (4 * fine)) / (2 * fine)
    zero = np.zeros_like(low)
    cosine = np.block([[np.cos(low), -np.sin(low)], [np.cos(high), np.sin(high)]])
    cosine_top = np.block([[np.cos(low), zero], [zero, np.cos(middle)]])
    sine = np.block([[np.sin(low), np.cos(low)], [np.sin(high), -np.cos(high)]])
    sine_top = np.block([[np.sin(low), zero], [zero, np.sin(middle)]])
    place = np.arange(fine)[None, :]
    index = np.where(place < half, k + 2 * coarse * place, 2 * coarse * (place - half + 1) - k)
    index[0] = np.where(place[0] < half, 2 * coarse * place[0], coarse + 2 * coarse * (place[0] - half))
    return first, turn, cosine, cosine_top, sine, sine_top, index


def spread(matrix, copies):
    size = matrix.shape[0]
    left = np.kron(np.eye(copies), matrix[:, :size])
    right = np.kron(np.eye(copies), matrix[:, size:])
    return np.concatenate([left, right], axis=1)


def parts(matrix):
    high = matrix.astype(np.float32).astype(ml_dtypes.bfloat16)
    low = (matrix - high.astype(np.float64)).astype(np.float32).astype(ml_dtypes.bfloat16)
    return [high, low]


def constants():
    first, turn, cosine, cosine_top, sine, sine_top, _ = tables(YA, YB)
    out = []
    high, low = parts(first)
    out += [np.concatenate([high, high, low], axis=1)]
    high, low = parts(first.T)
    out += [np.concatenate([high, high, low], axis=1)]
    out += [np.cos(turn).astype(np.float32), np.sin(turn).astype(np.float32)]
    out += parts(cosine.T) + parts(cosine_top.T)
    out += parts(cosine) + parts(cosine_top) + parts(sine) + parts(sine_top)
    first, turn, cosine, cosine_top, sine, sine_top, index = tables(XA, XB)
    copies = LANES // XB
    cosine, cosine_top, sine, sine_top = (spread(t, copies) for t in (cosine, cosine_top, sine, sine_top))
    out += parts(first) + parts(first.T)
    out += [np.tile(t, (1, copies)).astype(np.float32) for t in (np.cos(turn), np.sin(turn), index)]
    out += parts(cosine.T) + parts(cosine_top.T)
    out += parts(cosine) + parts(cosine_top) + parts(sine) + parts(sine_top)
    return out


def split(x):
    high = x.astype(BF16)
    return high, (x - high.astype(F32)).astype(BF16)


def dot(x, y):
    return jnp.dot(x, y, preferred_element_type=F32)


def times_table(x, table):
    high, low = split(x)
    t_high, t_low = table[0][...], table[1][...]
    return dot(high, t_high) + dot(low, t_high) + dot(high, t_low)


def table_times(table, x):
    high, low = split(x)
    t_high, t_low = table[0][...], table[1][...]
    return dot(t_high, high) + dot(t_high, low) + dot(t_low, high)


def kernel(*refs):
    counts, inverse = refs[:2]
    c = refs[2:-21]
    (
        out_first, out_second, density, buf, bc, bs, turned, send_x, recv_x, spec, spec_top, sum_top,
        send_y, recv_y, send_b, local_sem, sends, recv_sem_rows, recv_sem_x, recv_sem_y, recv_sem_b,
    ) = refs[-21:]
    y_first, y_first_t, y_cos, y_sin = c[0:4]
    y_second, y_second_top = c[4:6], c[6:8]
    y_sum = [c[8:10], c[12:14]]
    y_sum_top = [c[10:12], c[14:16]]
    x_first, x_first_t = c[16:18], c[18:20]
    x_cos, x_sin, x_index = c[20:23]
    x_second, x_second_top = c[23:25], c[25:27]
    x_sum = [c[31:33], c[27:29]]
    x_sum_top = [c[33:35], c[29:31]]
    outs = [out_first, out_second]

    row = lax.axis_index("row")
    col = lax.axis_index("col")
    me = row * COLS + col

    def place(device):
        return (device // COLS, device % COLS)

    def remote(src, dst, send, recv, device):
        return pltpu.make_async_remote_copy(
            src_ref=src, dst_ref=dst, send_sem=send, recv_sem=recv, device_id=device, device_id_type=MESH
        )

    barrier = pltpu.get_barrier_semaphore()

    def greet(j, _):
        pl.semaphore_signal(barrier, inc=1, device_id=place(lax.rem(me + j, DEVICES)), device_id_type=MESH)
        return 0

    lax.fori_loop(1, DEVICES, greet, 0)

    def make_density(t, _):
        owner, q = t // 4, t % 4
        at = pl.multiple_of(t * 8, 8)
        values = counts[pl.ds(at, 8), :].astype(F32) * inverse[pl.ds(at, 8), :] * 0.03125
        for tile in range(8):
            density[pl.ds(pl.multiple_of(t * 64 + tile * 8, 8), 8), :] = values[:, tile * LANES:(tile + 1) * LANES]
        return 0

    lax.fori_loop(0, 32, make_density, 0)
    pl.semaphore_wait(barrier, DEVICES - 1)

    def chunk(ref, at, size):
        return ref.at[pl.ds(pl.multiple_of(at, 8), size), :]

    own = []
    for q in range(4):
        copy = pltpu.make_async_copy(chunk(density, col * 256 + q * 64, 64), chunk(buf, q * 512 + col * 64, 64), local_sem.at[q])
        copy.start()
        own.append(copy)
        for j in range(1, COLS):
            other = lax.rem(col + j, COLS)
            remote(
                chunk(density, other * 256 + q * 64, 64), chunk(buf, q * 512 + col * 64, 64),
                sends.at[0], recv_sem_rows.at[q], (row, other),
            ).start()

    neighbour = (row, lax.rem(col + 1, COLS))

    for q in range(4):
        own[q].wait()
        whole = chunk(buf, 0, (COLS - 1) * 64)
        remote(whole, whole, sends.at[0], recv_sem_rows.at[q], neighbour).wait_recv()

        def first_y(p, _):
            at = q * 512 + 2 * p
            pair = jnp.concatenate(
                [buf[pl.ds(at, YA, stride=8), :], buf[pl.ds(at + 1, YA, stride=8), :]], axis=1
            )
            high, low = split(pair)
            result = dot(y_first[...], jnp.concatenate([high, low, high], axis=0))
            for e in range(2):
                i = q * 8 + 2 * p + e
                ac = result[:YA, e * LANES:(e + 1) * LANES]
                as_ = result[YA:, e * LANES:(e + 1) * LANES]
                bc[pl.ds(i, YA, stride=32), :] = ac * y_cos[...] - as_ * y_sin[...]
                bs[pl.ds(i, YA, stride=32), :] = ac * y_sin[...] + as_ * y_cos[...]
            return 0

        lax.fori_loop(0, 4, first_y, 0)

    def second_y(t, _):
        g = lax.rem(me // 16 + t, 16)
        at = pl.multiple_of(g * LANES, LANES)
        both = jnp.concatenate([bc[pl.ds(at, LANES), :], bs[pl.ds(at, LANES), :]], axis=1)
        turned[...] = times_table(both, y_second)

        @pl.when(g == 0)
        def _():
            turned[:32, :] = times_table(both[:32], y_second_top)

        send_x[pl.ds(at, LANES), :] = turned[...].T
        return 0

    lax.fori_loop(0, 16, second_y, 0)

    own = pltpu.make_async_copy(chunk(send_x, me * 8, 8), chunk(recv_x, me * 8, 8), local_sem.at[4])
    own.start()

    def send_tiles(src, dst, send, recv):
        def step(j, _):
            other = lax.rem(me + j, DEVICES)
            remote(chunk(src, other * 8, 8), chunk(dst, me * 8, 8), send, recv, place(other)).start()
            return 0

        lax.fori_loop(1, DEVICES, step, 0)

    most = (DEVICES - 1) * 8
    send_tiles(send_x, recv_x, sends.at[1], recv_sem_x)
    own.wait()
    remote(chunk(send_x, 0, most), chunk(recv_x, 0, most), sends.at[1], recv_sem_x, neighbour).wait_recv()

    def first_x(p, _):
        pair = jnp.concatenate(
            [recv_x[pl.ds(2 * p, XA, stride=8), :], recv_x[pl.ds(2 * p + 1, XA, stride=8), :]], axis=1
        )
        result = table_times(x_first, pair)
        for e in range(2):
            s = 2 * p + e
            ac = result[:XA, e * LANES:(e + 1) * LANES]
            as_ = result[XA:, e * LANES:(e + 1) * LANES]
            both = jnp.concatenate(
                [ac * x_cos[...] - as_ * x_sin[...], ac * x_sin[...] + as_ * x_cos[...]], axis=1
            )
            spec[pl.ds(pl.multiple_of(s * XA, XA), XA), :] = times_table(both, x_second)
            spec_top[pl.ds(s, 1), :] = both[:1]
        return 0

    lax.fori_loop(0, 4, first_x, 0)
    spec[pl.ds(0, 8, stride=XA), :] = times_table(spec_top[...], x_second_top)

    norming = 4.0 / math.sqrt(BINS * BINS) / math.pi

    def v_of(step, shape):
        lane = lax.broadcasted_iota(jnp.int32, shape, 1)
        k = 4 * (me // 16) + lane // XB
        l = 8 * lax.rem(me, 16) + step
        v_low = k + 2 * YA * l
        v_high = jnp.where(k == 0, 2 * YA * (l - YB // 2) + YA, 2 * YA * (l - YB // 2 + 1) - k)
        return jnp.where(l < YB // 2, v_low, v_high).astype(F32)

    def weigh(s, _):
        at = pl.multiple_of(s * XA, XA)
        v_row = v_of(s, (1, LANES))
        u = x_index[...]
        square = u * u + v_row * v_row
        corner = square == 0.0
        weight = jnp.where(corner, 0.0, norming / jnp.where(corner, 1.0, square))
        spec[pl.ds(at, XA), :] = spec[pl.ds(at, XA), :] * weight
        return 0

    lax.fori_loop(0, 8, weigh, 0)
    top = spec[pl.ds(0, 8, stride=XA), :]
    sum_top[0] = times_table(top * x_index[:1, :], x_sum_top[0])
    sum_top[1] = times_table(top * v_of(lax.broadcasted_iota(jnp.int32, (8, LANES), 0), (8, LANES)), x_sum_top[1])
    row_of = lax.broadcasted_iota(jnp.int32, (8, 2 * LANES), 0)

    own = []
    for f in range(2):

        def sum_x(p, _):
            halves = []
            for e in range(2):
                s = 2 * p + e
                value = spec[pl.ds(pl.multiple_of(s * XA, XA), XA), :]
                factor = x_index[...] if f == 0 else v_of(s, (1, LANES))
                result = times_table(value * factor, x_sum[f])
                head = jnp.sum(jnp.where(row_of == s, sum_top[f], 0.0), axis=0, keepdims=True)
                head = jnp.where(row_of == 0, head, result[:8])
                result = jnp.concatenate([head, result[8:]], axis=0)
                gc, gs = result[:, :LANES], result[:, LANES:]
                halves.append(
                    jnp.concatenate(
                        [gc * x_cos[...] + gs * x_sin[...], gs * x_cos[...] - gc * x_sin[...]], axis=0
                    )
                )
            result = table_times(x_first_t, jnp.concatenate(halves, axis=1))
            for e in range(2):
                send_y[f, pl.ds(2 * p + e, XA, stride=8), :] = result[:, e * LANES:(e + 1) * LANES]
            return 0

        lax.fori_loop(0, 4, sum_x, 0)
        copy = pltpu.make_async_copy(chunk(send_y.at[f], me * 8, 8), chunk(recv_y.at[f], me * 8, 8), local_sem.at[5 + f])
        copy.start()
        own.append(copy)
        send_tiles(send_y.at[f], recv_y.at[f], sends.at[2 + f], recv_sem_y.at[f])

    own_b = []
    for f in range(2):
        own[f].wait()
        remote(
            chunk(send_y.at[f], 0, most), chunk(recv_y.at[f], 0, most), sends.at[2 + f], recv_sem_y.at[f], neighbour
        ).wait_recv()

        def sum_y(g, _):
            at = pl.multiple_of(g * LANES, LANES)
            value = recv_y[f, pl.ds(at, LANES), :].T
            result = times_table(value, y_sum[f])
            bc[pl.ds(at, LANES), :] = result[:, :LANES]
            bs[pl.ds(at, LANES), :] = result[:, LANES:]

            @pl.when(g == 0)
            def _():
                result = times_table(value[:32], y_sum_top[f])
                bc[:32, :] = result[:, :LANES]
                bs[:32, :] = result[:, LANES:]

            return 0

        lax.fori_loop(0, 16, sum_y, 0)
        for q in range(4):

            def last_y(p, _):
                halves = []
                for e in range(2):
                    i = q * 8 + 2 * p + e
                    gc = bc[pl.ds(i, YA, stride=32), :]
                    gs = bs[pl.ds(i, YA, stride=32), :]
                    halves.append(
                        jnp.concatenate(
                            [gc * y_cos[...] + gs * y_sin[...], gs * y_cos[...] - gc * y_sin[...]], axis=0
                        )
                    )
                high, low = split(jnp.concatenate(halves, axis=1))
                result = dot(y_first_t[...], jnp.concatenate([high, low, high], axis=0))
                for e in range(2):
                    send_b[f, pl.ds(q * 512 + 2 * p + e, YA, stride=8), :] = result[:, e * LANES:(e + 1) * LANES]
                return 0

            lax.fori_loop(0, 4, last_y, 0)
            target = (4 * col + q) * 64
            copy = pltpu.make_async_copy(
                chunk(send_b.at[f], q * 512 + col * 64, 64), chunk(outs[f], target, 64), local_sem.at[7 + 4 * f + q]
            )
            copy.start()
            own_b.append(copy)
            for j in range(1, COLS):
                other = lax.rem(col + j, COLS)
                remote(
                    chunk(send_b.at[f], q * 512 + other * 64, 64), chunk(outs[f], target, 64),
                    sends.at[4 + f], recv_sem_b.at[f], (row, other),
                ).start()

    for copy in own_b:
        copy.wait()
    some = 4 * (COLS - 1) * 64
    for f in range(2):
        remote(chunk(send_b.at[f], 0, some), chunk(outs[f], 0, some), sends.at[4 + f], recv_sem_b.at[f], neighbour).wait()
        remote(chunk(send_y.at[f], 0, most), chunk(recv_y.at[f], 0, most), sends.at[2 + f], recv_sem_y.at[f], neighbour).wait_send()
    remote(chunk(send_x, 0, most), chunk(recv_x, 0, most), sends.at[1], recv_sem_x, neighbour).wait_send()
    remote(chunk(density, 0, some), chunk(buf, 0, some), sends.at[0], recv_sem_rows.at[0], neighbour).wait_send()


def on_device(counts, inverse_capacity):
    fixed = [jnp.asarray(table) for table in constants()]
    flat = (BINS // 4, LANES)
    vmem = pl.BlockSpec(memory_space=pltpu.VMEM)
    first, second = pl.pallas_call(
        kernel,
        out_shape=[jax.ShapeDtypeStruct(flat, F32)] * 2,
        in_specs=[vmem] * (2 + len(fixed)),
        out_specs=[vmem] * 2,
        scratch_shapes=[
            pltpu.VMEM(flat, F32),
            pltpu.VMEM(flat, F32),
            pltpu.VMEM(flat, F32),
            pltpu.VMEM(flat, F32),
            pltpu.VMEM((LANES, LANES), F32),
            pltpu.VMEM(flat, F32),
            pltpu.VMEM(flat, F32),
            pltpu.VMEM(flat, F32),
            pltpu.VMEM((8, 2 * LANES), F32),
            pltpu.VMEM((2, 8, 2 * LANES), F32),
            pltpu.VMEM((2,) + flat, F32),
            pltpu.VMEM((2,) + flat, F32),
            pltpu.VMEM((2,) + flat, F32),
            pltpu.SemaphoreType.DMA((15,)),
            pltpu.SemaphoreType.DMA((6,)),
            pltpu.SemaphoreType.DMA((4,)),
            pltpu.SemaphoreType.DMA,
            pltpu.SemaphoreType.DMA((2,)),
            pltpu.SemaphoreType.DMA((2,)),
        ],
        compiler_params=pltpu.CompilerParams(
            collective_id=0, has_side_effects=True, vmem_limit_bytes=48 * 2**20
        ),
        name="field",
    )(counts, inverse_capacity, *fixed)

    def blocked(x):
        return x.reshape(32, 8, 8, LANES).transpose(0, 2, 1, 3).reshape(256, 1024)

    return blocked(first), blocked(second)


def solution(mesh):
    return jax.shard_map(
        on_device,
        mesh=mesh,
        in_specs=(P("row", "col"), P("row", "col")),
        out_specs=(P("row", "col"), P("row", "col")),
        check_vma=False,
    )
```

```python
import math

import jax
import jax.numpy as jnp
import numpy as np
from jax import lax
from jax.experimental import pallas as pl
from jax.experimental.pallas import tpu as pltpu
from jax.sharding import PartitionSpec as P

MESH = pl.DeviceIdType.MESH
F32 = jnp.float32
BF16 = jnp.bfloat16
ROWS, COLS = 32, 8
DEVICES = ROWS * COLS
LANES = 128
YA, YB = 64, 128
XA, XB = 256, 32
BINS = 8192


def tables(coarse, fine):
    half = fine // 2
    k = np.arange(coarse)[:, None]
    a = np.arange(coarse)[None, :]
    angle = np.pi * (k * a % (2 * coarse)) / coarse
    first = np.concatenate([np.cos(angle), np.sin(angle)], axis=0)
    first[coarse] = 1.0 - 2.0 * (np.arange(coarse) % 2)
    odd = 2 * np.arange(fine)[None, :] + 1
    turn = np.pi * k * odd / (2 * coarse * fine)
    m = np.arange(half)[:, None]
    low = np.pi * (m * odd % (2 * fine)) / fine
    high = np.pi * ((m + 1) * odd % (2 * fine)) / fine
    middle = np.pi * ((2 * m + 1) * odd % (4 * fine)) / (2 * fine)
    zero = np.zeros_like(low)
    cosine = np.block([[np.cos(low), -np.sin(low)], [np.cos(high), np.sin(high)]])
    cosine_top = np.block([[np.cos(low), zero], [zero, np.cos(middle)]])
    sine = np.block([[np.sin(low), np.cos(low)], [np.sin(high), -np.cos(high)]])
    sine_top = np.block([[np.sin(low), zero], [zero, np.sin(middle)]])
    place = np.arange(fine)[None, :]
    index = np.where(place < half, k + 2 * coarse * place, 2 * coarse * (place - half + 1) - k)
    index[0] = np.where(place[0] < half, 2 * coarse * place[0], coarse + 2 * coarse * (place[0] - half))
    return first, turn, cosine, cosine_top, sine, sine_top, index


def spread(matrix, copies):
    size = matrix.shape[0]
    left = np.kron(np.eye(copies), matrix[:, :size])
    right = np.kron(np.eye(copies), matrix[:, size:])
    return np.concatenate([left, right], axis=1)


def constants():
    products, singles = [], []
    first, turn, cosine, cosine_top, sine, sine_top, _ = tables(YA, YB)
    products += [("y_first", np.concatenate([first, np.zeros_like(first)], axis=1)), ("y_first_t", first.T)]
    singles += [("y_cos", np.cos(turn)), ("y_sin", np.sin(turn))]

    def seconds(axis, cosine, cosine_top, sine, sine_top):
        found = [(axis + "_second", cosine.T), (axis + "_second_top", cosine_top.T)]
        for name, table in (("_cos", cosine), ("_cos_top", cosine_top), ("_sin", sine), ("_sin_top", sine_top)):
            found += [(axis + name, table)]
        return found

    products += seconds("y", cosine, cosine_top, sine, sine_top)
    first, turn, cosine, cosine_top, sine, sine_top, index = tables(XA, XB)
    copies = LANES // XB
    products += [("x_first", first), ("x_first_t", first.T)]
    singles += [(name, np.tile(t, (1, copies))) for name, t in
                (("x_cos", np.cos(turn)), ("x_sin", np.sin(turn)), ("x_index", index))]
    products += seconds("x", *(spread(t, copies) for t in (cosine, cosine_top, sine, sine_top)))

    def pack(named):
        at, places = 0, {}
        for name, table in named:
            places[name] = (at, table.shape)
            at += table.size // LANES
        tiled = [
            table[:, lane:lane + LANES] for _, table in named for lane in range(0, table.shape[1], LANES)
        ]
        return np.concatenate(tiled, axis=0).astype(np.float32), places

    return pack(products) + pack(singles)


PRODUCTS, PRODUCT_AT, SINGLES, SINGLE_AT = constants()


def split(x):
    high = x.astype(BF16)
    return high, (x - high.astype(F32)).astype(BF16)


def dot(x, y):
    return jnp.dot(x, y, preferred_element_type=F32)


def times_table(x, table):
    high, low = split(x)
    t_high, t_low = table()
    return dot(high, t_high) + dot(low, t_high) + dot(high, t_low)


def table_times(table, x):
    high, low = split(x)
    t_high, t_low = table()
    return dot(t_high, high) + dot(t_high, low) + dot(t_low, high)


def kernel(
    counts_hbm, inverse_hbm, products_hbm, singles_hbm, out_first, out_second,
    counts, inverse, products, singles, table_high, table_low, y_stack, density, buf, bc, bs, turned, send_x, recv_x, spec, spec_top, sum_top,
    send_y, recv_y, send_b, load_sem, local_sem, sends, recv_sem_rows, recv_sem_x, recv_sem_y, recv_sem_b,
):
    def single(name):
        at, (height, _) = SINGLE_AT[name]
        return singles[at:at + height, :]

    def table(name):
        at, (height, width) = PRODUCT_AT[name]
        return lambda: [
            jnp.concatenate([part[at + t * height:at + (t + 1) * height, :] for t in range(width // LANES)], axis=1)
            for part in (table_high, table_low)
        ]

    outs = [out_first, out_second]
    pending = []
    loads = [
        pltpu.make_async_copy(counts_hbm, counts, load_sem.at[0]),
        pltpu.make_async_copy(inverse_hbm, inverse, load_sem.at[1]),
        pltpu.make_async_copy(products_hbm, products, load_sem.at[2]),
        pltpu.make_async_copy(singles_hbm, singles, load_sem.at[3]),
    ]
    for copy in loads:
        copy.start()

    row = lax.axis_index("row")
    col = lax.axis_index("col")
    me = row * COLS + col

    def place(device):
        return (device // COLS, device % COLS)

    def remote(src, dst, send, recv, device):
        return pltpu.make_async_remote_copy(
            src_ref=src, dst_ref=dst, send_sem=send, recv_sem=recv, device_id=device, device_id_type=MESH
        )

    barrier = pltpu.get_barrier_semaphore()

    for j in range(1, COLS):
        pl.semaphore_signal(barrier, inc=1, device_id=(row, lax.rem(col + j, COLS)), device_id_type=MESH)

    def greet(j, _):
        pl.semaphore_signal(barrier, inc=1, device_id=(lax.rem(row + j, ROWS), col), device_id_type=MESH)
        return 0

    lax.fori_loop(1, ROWS, greet, 0)

    loads[0].wait()
    loads[1].wait()

    def make_density(t, _):
        owner, q = t // 4, t % 4
        at = pl.multiple_of(t * 8, 8)
        values = counts[pl.ds(at, 8), :].astype(F32) * inverse[pl.ds(at, 8), :] * 0.03125
        for tile in range(8):
            density[pl.ds(pl.multiple_of(t * 64 + tile * 8, 8), 8), :] = values[:, tile * LANES:(tile + 1) * LANES]
        return 0

    lax.fori_loop(0, 32, make_density, 0)
    pl.semaphore_wait(barrier, ROWS + COLS - 2)

    def chunk(ref, at, size):
        return ref.at[pl.ds(pl.multiple_of(at, 8), size), :]

    own = []
    for q in range(4):
        copy = pltpu.make_async_copy(chunk(density, col * 256 + q * 64, 64), chunk(buf, q * 512 + col * 64, 64), local_sem.at[q])
        copy.start()
        own.append(copy)
        for j in range(1, COLS):
            other = lax.rem(col + j, COLS)
            remote(
                chunk(density, other * 256 + q * 64, 64), chunk(buf, q * 512 + col * 64, 64),
                sends.at[0], recv_sem_rows.at[q], (row, other),
            ).start()

    neighbour = (row, lax.rem(col + 1, COLS))

    loads[2].wait()
    loads[3].wait()

    def split_tables(t, _):
        at = pl.ds(pl.multiple_of(t * 64, 64), 64)
        table_high[at, :], table_low[at, :] = split(products[at, :])
        return 0

    lax.fori_loop(0, PRODUCTS.shape[0] // 64, split_tables, 0)
    high, low = (part[:, :YA] for part in table("y_first")())
    y_stack[...] = jnp.concatenate([high, high, low], axis=1)
    for q in range(4):
        own[q].wait()
        whole = chunk(buf, 0, (COLS - 1) * 64)
        remote(whole, whole, sends.at[0], recv_sem_rows.at[q], neighbour).wait_recv()

        def first_y(p, _):
            at = q * 512 + 2 * p
            pair = jnp.concatenate(
                [buf[pl.ds(at, YA, stride=8), :], buf[pl.ds(at + 1, YA, stride=8), :]], axis=1
            )
            high, low = split(pair)
            result = dot(y_stack[...], jnp.concatenate([high, low, high], axis=0))
            for e in range(2):
                i = q * 8 + 2 * p + e
                ac = result[:YA, e * LANES:(e + 1) * LANES]
                as_ = result[YA:, e * LANES:(e + 1) * LANES]
                bc[pl.ds(i, YA, stride=32), :] = ac * single("y_cos") - as_ * single("y_sin")
                bs[pl.ds(i, YA, stride=32), :] = ac * single("y_sin") + as_ * single("y_cos")
            return 0

        lax.fori_loop(0, 4, first_y, 0)

    def second_y(t, _):
        at = pl.multiple_of(t * 512, 512)
        both = jnp.concatenate([bc[pl.ds(at, 512), :], bs[pl.ds(at, 512), :]], axis=1)
        turned[...] = times_table(both, table("y_second"))

        @pl.when(t == 0)
        def _():
            turned[:32, :] = times_table(both[:32], table("y_second_top"))

        for g in range(4):
            block = turned[g * LANES:(g + 1) * LANES, :].T
            for h in range(2):
                send_x.at[h].reshape(1024, LANES)[pl.ds(pl.multiple_of(t * 256 + g * 64, 64), 64), :] = block[h * 64:(h + 1) * 64]
        return 0

    lax.fori_loop(0, 4, second_y, 0)

    def exchange(src, dst, send, recv, local):
        copy = pltpu.make_async_copy(src.at[me], dst.at[me], local)
        copy.start()

        def step(j, _):
            for e in range(5):
                other = lax.rem(me + 1 + 5 * j + e, DEVICES)
                remote(src.at[other], dst.at[me], send, recv, place(other)).start()
            return 0

        lax.fori_loop(0, (DEVICES - 1) // 5, step, 0)
        rest = remote(src.at[pl.ds(0, DEVICES - 1)], dst.at[pl.ds(0, DEVICES - 1)], send, recv, neighbour)
        pending.append(rest.wait_send)

        def arrived():
            copy.wait()
            rest.wait_recv()

        return arrived

    arrived_x = [
        exchange(send_x.at[h], recv_x.at[h], sends.at[1 + h], recv_sem_x.at[h], local_sem.at[4 + h]) for h in range(2)
    ]
    spec_top[...] = jnp.zeros_like(spec_top)
    row_of = lax.broadcasted_iota(jnp.int32, (8, 2 * LANES), 0)
    norming = 4.0 / math.sqrt(BINS * BINS) / math.pi

    def v_of(half, step, shape):
        k = 4 * (me // 16) + lax.broadcasted_iota(jnp.int32, shape, 1) // XB
        m = 4 * lax.rem(me, 16) + step
        if half == 0:
            return (k + 2 * YA * m).astype(F32)
        return jnp.where(k == 0, 2 * YA * m + YA, 2 * YA * (m + 1) - k).astype(F32)

    arrived_y = {}
    for h in range(2):
        arrived_x[h]()
        pieces = recv_x.at[h].reshape(1024, LANES)

        def first_x(p, _):
            pair = jnp.concatenate(
                [pieces[pl.ds(2 * p, XA, stride=4), :], pieces[pl.ds(2 * p + 1, XA, stride=4), :]], axis=1
            )
            result = table_times(table("x_first"), pair)
            for e in range(2):
                s = 2 * p + e
                ac = result[:XA, e * LANES:(e + 1) * LANES]
                as_ = result[XA:, e * LANES:(e + 1) * LANES]
                both = jnp.concatenate(
                    [ac * single("x_cos") - as_ * single("x_sin"), ac * single("x_sin") + as_ * single("x_cos")],
                    axis=1,
                )
                spec[pl.ds(pl.multiple_of(s * XA, XA), XA), :] = times_table(both, table("x_second"))
                spec_top[pl.ds(s, 1), :] = both[:1]
            return 0

        lax.fori_loop(0, 2, first_x, 0)
        spec[pl.ds(0, 4, stride=XA), :] = times_table(spec_top[...], table("x_second_top"))[:4]

        def weigh(s, _):
            at = pl.multiple_of(s * XA, XA)
            v_row = v_of(h, s, (1, LANES))
            u = single("x_index")
            square = u * u + v_row * v_row
            corner = square == 0.0
            weight = jnp.where(corner, 0.0, norming / jnp.where(corner, 1.0, square))
            spec[pl.ds(at, XA), :] = spec[pl.ds(at, XA), :] * weight
            return 0

        lax.fori_loop(0, 4, weigh, 0)
        top = spec[pl.ds(0, 4, stride=XA), :]
        top = jnp.concatenate([top, jnp.zeros_like(top)], axis=0)
        tops = [
            times_table(top * single("x_index")[:1], table("x_sin_top")),
            times_table(top * v_of(h, lax.broadcasted_iota(jnp.int32, (8, LANES), 0), (8, LANES)), table("x_cos_top")),
        ]
        for f in range(2):
            sum_top[f] = tops[f]

        for f in range(2):
            target = send_y.at[f, h].reshape(1024, LANES)

            def sum_x(p, _):
                both = []
                for e in range(2):
                    s = 2 * p + e
                    value = spec[pl.ds(pl.multiple_of(s * XA, XA), XA), :]
                    factor = single("x_index") if f == 0 else v_of(h, s, (1, LANES))
                    result = times_table(value * factor, table(("x_sin", "x_cos")[f]))
                    head = jnp.sum(jnp.where(row_of == s, sum_top[f], 0.0), axis=0, keepdims=True)
                    head = jnp.where(row_of == 0, head, result[:8])
                    result = jnp.concatenate([head, result[8:]], axis=0)
                    gc, gs = result[:, :LANES], result[:, LANES:]
                    both.append(
                        jnp.concatenate(
                            [gc * single("x_cos") + gs * single("x_sin"), gs * single("x_cos") - gc * single("x_sin")],
                            axis=0,
                        )
                    )
                result = table_times(table("x_first_t"), jnp.concatenate(both, axis=1))
                for e in range(2):
                    target[pl.ds(2 * p + e, XA, stride=4), :] = result[:, e * LANES:(e + 1) * LANES]
                return 0

            lax.fori_loop(0, 2, sum_x, 0)
            arrived_y[f, h] = exchange(
                send_y.at[f, h], recv_y.at[f, h], sends.at[3 + 2 * f + h], recv_sem_y.at[2 * f + h],
                local_sem.at[6 + 2 * f + h],
            )

    for f in range(2):
        for h in range(2):
            arrived_y[f, h]()

        def sum_y(g, _):
            at = pl.multiple_of(g * LANES, LANES)
            half = pl.ds(pl.multiple_of(g * 64, 64), 64)
            value = jnp.concatenate([recv_y.at[f, h].reshape(1024, LANES)[half, :] for h in range(2)], axis=0).T
            result = times_table(value, table(("y_cos", "y_sin")[f]))
            bc[pl.ds(at, LANES), :] = result[:, :LANES]
            bs[pl.ds(at, LANES), :] = result[:, LANES:]

            @pl.when(g == 0)
            def _():
                result = times_table(value[:32], table(("y_cos_top", "y_sin_top")[f]))
                bc[:32, :] = result[:, :LANES]
                bs[:32, :] = result[:, LANES:]

            return 0

        lax.fori_loop(0, 16, sum_y, 0)
        for q in range(4):

            def last_y(p, _):
                both = []
                for e in range(2):
                    i = q * 8 + 2 * p + e
                    gc = bc[pl.ds(i, YA, stride=32), :]
                    gs = bs[pl.ds(i, YA, stride=32), :]
                    both.append(
                        jnp.concatenate(
                            [gc * single("y_cos") + gs * single("y_sin"), gs * single("y_cos") - gc * single("y_sin")], axis=0
                        )
                    )
                result = table_times(table("y_first_t"), jnp.concatenate(both, axis=1))
                for e in range(2):
                    send_b[f, pl.ds(q * 512 + 2 * p + e, YA, stride=8), :] = result[:, e * LANES:(e + 1) * LANES]
                return 0

            lax.fori_loop(0, 4, last_y, 0)
            target = (4 * col + q) * 64
            copy = pltpu.make_async_copy(
                chunk(send_b.at[f], q * 512 + col * 64, 64), chunk(outs[f], target, 64), local_sem.at[10 + 4 * f + q]
            )
            copy.start()
            pending.append(copy.wait)
            for j in range(1, COLS):
                other = lax.rem(col + j, COLS)
                remote(
                    chunk(send_b.at[f], q * 512 + other * 64, 64), chunk(outs[f], target, 64),
                    sends.at[7 + f], recv_sem_b.at[f], (row, other),
                ).start()

    some = 4 * (COLS - 1) * 64
    for f in range(2):
        remote(chunk(send_b.at[f], 0, some), chunk(outs[f], 0, some), sends.at[7 + f], recv_sem_b.at[f], neighbour).wait()
    remote(chunk(density, 0, some), chunk(buf, 0, some), sends.at[0], recv_sem_rows.at[0], neighbour).wait_send()
    for wait in pending:
        wait()


def on_device(counts, inverse_capacity):
    flat = (BINS // 4, LANES)
    vmem = pl.BlockSpec(memory_space=pltpu.VMEM)
    hbm = pl.BlockSpec(memory_space=pltpu.HBM)
    first, second = pl.pallas_call(
        kernel,
        out_shape=[jax.ShapeDtypeStruct(flat, F32)] * 2,
        in_specs=[hbm] * 4,
        out_specs=[vmem] * 2,
        scratch_shapes=[
            pltpu.VMEM(counts.shape, jnp.int32),
            pltpu.VMEM(counts.shape, F32),
            pltpu.VMEM(PRODUCTS.shape, F32),
            pltpu.VMEM(SINGLES.shape, F32),
            pltpu.VMEM(PRODUCTS.shape, BF16),
            pltpu.VMEM(PRODUCTS.shape, BF16),
            pltpu.VMEM((2 * YA, 3 * YA), BF16),
            pltpu.VMEM(flat, F32),
            pltpu.VMEM(flat, F32),
            pltpu.VMEM(flat, F32),
            pltpu.VMEM(flat, F32),
            pltpu.VMEM((4 * LANES, LANES), F32),
            pltpu.VMEM((2, DEVICES, 4, LANES), F32),
            pltpu.VMEM((2, DEVICES, 4, LANES), F32),
            pltpu.VMEM((1024, LANES), F32),
            pltpu.VMEM((8, 2 * LANES), F32),
            pltpu.VMEM((2, 8, 2 * LANES), F32),
            pltpu.VMEM((2, 2, DEVICES, 4, LANES), F32),
            pltpu.VMEM((2, 2, DEVICES, 4, LANES), F32),
            pltpu.VMEM((2,) + flat, F32),
            pltpu.SemaphoreType.DMA((4,)),
            pltpu.SemaphoreType.DMA((18,)),
            pltpu.SemaphoreType.DMA((9,)),
            pltpu.SemaphoreType.DMA((4,)),
            pltpu.SemaphoreType.DMA((2,)),
            pltpu.SemaphoreType.DMA((4,)),
            pltpu.SemaphoreType.DMA((2,)),
        ],
        compiler_params=pltpu.CompilerParams(
            collective_id=0, has_side_effects=True, vmem_limit_bytes=58 * 2**20
        ),
        name="field",
    )(counts, inverse_capacity, jnp.asarray(PRODUCTS), jnp.asarray(SINGLES))

    def blocked(x):
        return x.reshape(32, 8, 8, LANES).transpose(0, 2, 1, 3).reshape(256, 1024)

    return blocked(first), blocked(second)


def solution(mesh):
    return jax.shard_map(
        on_device,
        mesh=mesh,
        in_specs=(P("row", "col"), P("row", "col")),
        out_specs=(P("row", "col"), P("row", "col")),
        check_vma=False,
    )
```

```python
import math

import jax
import jax.numpy as jnp
import numpy as np
from jax import lax
from jax.experimental import pallas as pl
from jax.experimental.pallas import tpu as pltpu
from jax.sharding import PartitionSpec as P

MESH = pl.DeviceIdType.MESH
F32 = jnp.float32
BF16 = jnp.bfloat16
ROWS, COLS = 32, 8
DEVICES = ROWS * COLS
LANES = 128
YA, YB = 64, 128
XA, XB = 256, 32
BINS = 8192


def tables(coarse, fine):
    half = fine // 2
    k = np.arange(coarse)[:, None]
    a = np.arange(coarse)[None, :]
    angle = np.pi * (k * a % (2 * coarse)) / coarse
    first = np.concatenate([np.cos(angle), np.sin(angle)], axis=0)
    first[coarse] = 1.0 - 2.0 * (np.arange(coarse) % 2)
    odd = 2 * np.arange(fine)[None, :] + 1
    turn = np.pi * k * odd / (2 * coarse * fine)
    m = np.arange(half)[:, None]
    low = np.pi * (m * odd % (2 * fine)) / fine
    high = np.pi * ((m + 1) * odd % (2 * fine)) / fine
    middle = np.pi * ((2 * m + 1) * odd % (4 * fine)) / (2 * fine)
    zero = np.zeros_like(low)
    cosine = np.block([[np.cos(low), -np.sin(low)], [np.cos(high), np.sin(high)]])
    cosine_top = np.block([[np.cos(low), zero], [zero, np.cos(middle)]])
    sine = np.block([[np.sin(low), np.cos(low)], [np.sin(high), -np.cos(high)]])
    sine_top = np.block([[np.sin(low), zero], [zero, np.sin(middle)]])
    place = np.arange(fine)[None, :]
    index = np.where(place < half, k + 2 * coarse * place, 2 * coarse * (place - half + 1) - k)
    index[0] = np.where(place[0] < half, 2 * coarse * place[0], coarse + 2 * coarse * (place[0] - half))
    return first, turn, cosine, cosine_top, sine, sine_top, index


def spread(matrix, copies):
    size = matrix.shape[0]
    left = np.kron(np.eye(copies), matrix[:, :size])
    right = np.kron(np.eye(copies), matrix[:, size:])
    return np.concatenate([left, right], axis=1)


def constants():
    products, singles = [], []
    first, turn, cosine, cosine_top, sine, sine_top, _ = tables(YA, YB)
    products += [("y_first", np.concatenate([first, np.zeros_like(first)], axis=1)), ("y_first_t", first.T)]
    singles += [("y_cos", np.cos(turn)), ("y_sin", np.sin(turn))]

    def seconds(axis, cosine, cosine_top, sine, sine_top):
        found = [(axis + "_second", cosine.T), (axis + "_second_top", cosine_top.T)]
        for name, table in (("_cos", cosine), ("_cos_top", cosine_top), ("_sin", sine), ("_sin_top", sine_top)):
            found += [(axis + name, table)]
        return found

    products += seconds("y", cosine, cosine_top, sine, sine_top)
    first, turn, cosine, cosine_top, sine, sine_top, index = tables(XA, XB)
    copies = LANES // XB
    products += [("x_first", first), ("x_first_t", first.T)]
    singles += [(name, np.tile(t, (1, copies))) for name, t in
                (("x_cos", np.cos(turn)), ("x_sin", np.sin(turn)), ("x_index", index))]
    products += seconds("x", *(spread(t, copies) for t in (cosine, cosine_top, sine, sine_top)))

    def pack(named):
        at, places = 0, {}
        for name, table in named:
            places[name] = (at, table.shape)
            at += table.size // LANES
        tiled = [
            table[:, lane:lane + LANES] for _, table in named for lane in range(0, table.shape[1], LANES)
        ]
        return np.concatenate(tiled, axis=0).astype(np.float32), places

    return pack(products) + pack(singles)


PRODUCTS, PRODUCT_AT, SINGLES, SINGLE_AT = constants()


def split(x):
    high = x.astype(BF16)
    return high, (x - high.astype(F32)).astype(BF16)


def dot(x, y):
    return jnp.dot(x, y, preferred_element_type=F32)


def times_table(x, table):
    high, low = split(x)
    t_high, t_low = table()
    return dot(high, t_high) + dot(low, t_high) + dot(high, t_low)


def table_times(table, x):
    high, low = split(x)
    t_high, t_low = table()
    return dot(t_high, high) + dot(t_high, low) + dot(t_low, high)


def kernel(
    counts_hbm, inverse_hbm, products_hbm, singles_hbm, out_first, out_second,
    counts, inverse, products, singles, table_high, table_low, y_stack, density, buf, bc, bs, turned, send_x, recv_x, spec, spec_top, sum_top,
    send_y, recv_y, send_b, load_sem, local_sem, sends, recv_sem_rows, recv_sem_x, recv_sem_y, recv_sem_b,
):
    def single(name):
        at, (height, _) = SINGLE_AT[name]
        return singles[at:at + height, :]

    def table(name):
        at, (height, width) = PRODUCT_AT[name]
        return lambda: [
            jnp.concatenate([part[at + t * height:at + (t + 1) * height, :] for t in range(width // LANES)], axis=1)
            for part in (table_high, table_low)
        ]

    outs = [out_first, out_second]
    pending = []
    loads = [
        pltpu.make_async_copy(counts_hbm, counts, load_sem.at[0]),
        pltpu.make_async_copy(inverse_hbm, inverse, load_sem.at[1]),
        pltpu.make_async_copy(products_hbm, products, load_sem.at[2]),
        pltpu.make_async_copy(singles_hbm, singles, load_sem.at[3]),
    ]
    for copy in loads:
        copy.start()

    row = lax.axis_index("row")
    col = lax.axis_index("col")
    me = row * COLS + col

    def place(device):
        return (device // COLS, device % COLS)

    def remote(src, dst, send, recv, device):
        return pltpu.make_async_remote_copy(
            src_ref=src, dst_ref=dst, send_sem=send, recv_sem=recv, device_id=device, device_id_type=MESH
        )

    barrier = pltpu.get_barrier_semaphore()

    for j in range(1, COLS):
        pl.semaphore_signal(barrier, inc=1, device_id=(row, lax.rem(col + j, COLS)), device_id_type=MESH)

    def greet(j, _):
        pl.semaphore_signal(barrier, inc=1, device_id=(lax.rem(row + j, ROWS), col), device_id_type=MESH)
        return 0

    lax.fori_loop(1, ROWS, greet, 0)

    loads[0].wait()
    loads[1].wait()

    def chunk(ref, at, size):
        return ref.at[pl.ds(pl.multiple_of(at, 8), size), :]

    own = []
    for q in range(4):

        def make_density(owner, _):
            at = pl.multiple_of(owner * 32 + q * 8, 8)
            values = counts[pl.ds(at, 8), :].astype(F32) * inverse[pl.ds(at, 8), :] * 0.03125
            for tile in range(8):
                to = pl.multiple_of(owner * 256 + q * 64 + tile * 8, 8)
                density[pl.ds(to, 8), :] = values[:, tile * LANES:(tile + 1) * LANES]
            return 0

        lax.fori_loop(0, 8, make_density, 0)
        if q == 0:
            pl.semaphore_wait(barrier, ROWS + COLS - 2)

        copy = pltpu.make_async_copy(
            chunk(density, col * 256 + q * 64, 64), chunk(buf, q * 512 + col * 64, 64), local_sem.at[q]
        )
        copy.start()
        own.append(copy)
        for j in range(1, COLS):
            other = lax.rem(col + j, COLS)
            remote(
                chunk(density, other * 256 + q * 64, 64), chunk(buf, q * 512 + col * 64, 64),
                sends.at[0], recv_sem_rows.at[q], (row, other),
            ).start()

    neighbour = (row, lax.rem(col + 1, COLS))

    loads[2].wait()
    loads[3].wait()

    def split_tables(t, _):
        at = pl.ds(pl.multiple_of(t * 64, 64), 64)
        table_high[at, :], table_low[at, :] = split(products[at, :])
        return 0

    lax.fori_loop(0, PRODUCTS.shape[0] // 64, split_tables, 0)
    high, low = (part[:, :YA] for part in table("y_first")())
    y_stack[...] = jnp.concatenate([high, high, low], axis=1)
    for q in range(4):
        own[q].wait()
        whole = chunk(buf, 0, (COLS - 1) * 64)
        remote(whole, whole, sends.at[0], recv_sem_rows.at[q], neighbour).wait_recv()

        def first_y(p, _):
            at = q * 512 + 2 * p
            pair = jnp.concatenate(
                [buf[pl.ds(at, YA, stride=8), :], buf[pl.ds(at + 1, YA, stride=8), :]], axis=1
            )
            high, low = split(pair)
            result = dot(y_stack[...], jnp.concatenate([high, low, high], axis=0))
            for e in range(2):
                i = q * 8 + 2 * p + e
                ac = result[:YA, e * LANES:(e + 1) * LANES]
                as_ = result[YA:, e * LANES:(e + 1) * LANES]
                bc[pl.ds(i, YA, stride=32), :] = ac * single("y_cos") - as_ * single("y_sin")
                bs[pl.ds(i, YA, stride=32), :] = ac * single("y_sin") + as_ * single("y_cos")
            return 0

        lax.fori_loop(0, 4, first_y, 0)

    def send_piece(src, dst, send, recv, other):
        remote(src.at[other], dst.at[me], send, recv, place(other)).start()

    def settle(src, dst, send, recv, local):
        copy = pltpu.make_async_copy(src.at[me], dst.at[me], local)
        copy.start()
        rest = remote(src.at[pl.ds(0, DEVICES - 1)], dst.at[pl.ds(0, DEVICES - 1)], send, recv, neighbour)
        pending.append(rest.wait_send)

        def arrived():
            copy.wait()
            rest.wait_recv()

        return arrived

    def exchange(src, dst, send, recv, local):
        def step(j, _):
            for e in range(5):
                send_piece(src, dst, send, recv, lax.rem(me + 1 + 5 * j + e, DEVICES))
            return 0

        lax.fori_loop(0, (DEVICES - 1) // 5, step, 0)
        return settle(src, dst, send, recv, local)

    channel = [
        (send_x.at[h], recv_x.at[h], sends.at[1 + h], recv_sem_x.at[h], local_sem.at[4 + h]) for h in range(2)
    ]

    def second_y(t, _):
        first = lax.rem(me // 64 + t, 4)
        at = pl.multiple_of(first * 512, 512)
        both = jnp.concatenate([bc[pl.ds(at, 512), :], bs[pl.ds(at, 512), :]], axis=1)
        turned[...] = times_table(both, table("y_second"))

        @pl.when(first == 0)
        def _():
            turned[:32, :] = times_table(both[:32], table("y_second_top"))

        for g in range(4):
            block = turned[g * LANES:(g + 1) * LANES, :].T
            for h in range(2):
                to = pl.multiple_of(first * 256 + g * 64, 64)
                send_x.at[h].reshape(1024, LANES)[pl.ds(to, 64), :] = block[h * 64:(h + 1) * 64]

        def step(other, _):
            send_piece(*channel[0][:4], other)
            return 0

        lax.fori_loop(jnp.where(t == 0, me + 1, first * 64), first * 64 + 64, step, 0)
        return 0

    lax.fori_loop(0, 4, second_y, 0)

    def rest_of_own(other, _):
        send_piece(*channel[0][:4], other)
        return 0

    lax.fori_loop(me // 64 * 64, me, rest_of_own, 0)
    arrived_x = [settle(*channel[0]), exchange(*channel[1])]
    spec_top[...] = jnp.zeros_like(spec_top)
    row_of = lax.broadcasted_iota(jnp.int32, (8, 2 * LANES), 0)
    norming = 4.0 / math.sqrt(BINS * BINS) / math.pi

    def v_of(half, step, shape):
        k = 4 * (me // 16) + lax.broadcasted_iota(jnp.int32, shape, 1) // XB
        m = 4 * lax.rem(me, 16) + step
        if half == 0:
            return (k + 2 * YA * m).astype(F32)
        return jnp.where(k == 0, 2 * YA * m + YA, 2 * YA * (m + 1) - k).astype(F32)

    arrived_y = {}
    for h in range(2):
        arrived_x[h]()
        pieces = recv_x.at[h].reshape(1024, LANES)

        def first_x(p, _):
            pair = jnp.concatenate(
                [pieces[pl.ds(2 * p, XA, stride=4), :], pieces[pl.ds(2 * p + 1, XA, stride=4), :]], axis=1
            )
            result = table_times(table("x_first"), pair)
            for e in range(2):
                s = 2 * p + e
                ac = result[:XA, e * LANES:(e + 1) * LANES]
                as_ = result[XA:, e * LANES:(e + 1) * LANES]
                both = jnp.concatenate(
                    [ac * single("x_cos") - as_ * single("x_sin"), ac * single("x_sin") + as_ * single("x_cos")],
                    axis=1,
                )
                spec[pl.ds(pl.multiple_of(s * XA, XA), XA), :] = times_table(both, table("x_second"))
                spec_top[pl.ds(s, 1), :] = both[:1]
            return 0

        lax.fori_loop(0, 2, first_x, 0)
        spec[pl.ds(0, 4, stride=XA), :] = times_table(spec_top[...], table("x_second_top"))[:4]

        def weigh(s, _):
            at = pl.multiple_of(s * XA, XA)
            v_row = v_of(h, s, (1, LANES))
            u = single("x_index")
            square = u * u + v_row * v_row
            corner = square == 0.0
            weight = jnp.where(corner, 0.0, norming / jnp.where(corner, 1.0, square))
            spec[pl.ds(at, XA), :] = spec[pl.ds(at, XA), :] * weight
            return 0

        lax.fori_loop(0, 4, weigh, 0)
        top = spec[pl.ds(0, 4, stride=XA), :]
        top = jnp.concatenate([top, jnp.zeros_like(top)], axis=0)
        tops = [
            times_table(top * single("x_index")[:1], table("x_sin_top")),
            times_table(top * v_of(h, lax.broadcasted_iota(jnp.int32, (8, LANES), 0), (8, LANES)), table("x_cos_top")),
        ]
        for f in range(2):
            sum_top[f] = tops[f]

        for f in range(2):
            target = send_y.at[f, h].reshape(1024, LANES)

            def sum_x(p, _):
                both = []
                for e in range(2):
                    s = 2 * p + e
                    value = spec[pl.ds(pl.multiple_of(s * XA, XA), XA), :]
                    factor = single("x_index") if f == 0 else v_of(h, s, (1, LANES))
                    result = times_table(value * factor, table(("x_sin", "x_cos")[f]))
                    head = jnp.sum(jnp.where(row_of == s, sum_top[f], 0.0), axis=0, keepdims=True)
                    head = jnp.where(row_of == 0, head, result[:8])
                    result = jnp.concatenate([head, result[8:]], axis=0)
                    gc, gs = result[:, :LANES], result[:, LANES:]
                    both.append(
                        jnp.concatenate(
                            [gc * single("x_cos") + gs * single("x_sin"), gs * single("x_cos") - gc * single("x_sin")],
                            axis=0,
                        )
                    )
                result = table_times(table("x_first_t"), jnp.concatenate(both, axis=1))
                for e in range(2):
                    target[pl.ds(2 * p + e, XA, stride=4), :] = result[:, e * LANES:(e + 1) * LANES]
                return 0

            lax.fori_loop(0, 2, sum_x, 0)
            arrived_y[f, h] = exchange(
                send_y.at[f, h], recv_y.at[f, h], sends.at[3 + 2 * f + h], recv_sem_y.at[2 * f + h],
                local_sem.at[6 + 2 * f + h],
            )

    for f in range(2):
        for h in range(2):
            arrived_y[f, h]()

        def sum_y(g, _):
            at = pl.multiple_of(g * LANES, LANES)
            half = pl.ds(pl.multiple_of(g * 64, 64), 64)
            value = jnp.concatenate([recv_y.at[f, h].reshape(1024, LANES)[half, :] for h in range(2)], axis=0).T
            result = times_table(value, table(("y_cos", "y_sin")[f]))
            bc[pl.ds(at, LANES), :] = result[:, :LANES]
            bs[pl.ds(at, LANES), :] = result[:, LANES:]

            @pl.when(g == 0)
            def _():
                result = times_table(value[:32], table(("y_cos_top", "y_sin_top")[f]))
                bc[:32, :] = result[:, :LANES]
                bs[:32, :] = result[:, LANES:]

            return 0

        lax.fori_loop(0, 16, sum_y, 0)
        for q in range(4):

            def last_y(p, _):
                both = []
                for e in range(2):
                    i = q * 8 + 2 * p + e
                    gc = bc[pl.ds(i, YA, stride=32), :]
                    gs = bs[pl.ds(i, YA, stride=32), :]
                    both.append(
                        jnp.concatenate(
                            [gc * single("y_cos") + gs * single("y_sin"), gs * single("y_cos") - gc * single("y_sin")], axis=0
                        )
                    )
                result = table_times(table("y_first_t"), jnp.concatenate(both, axis=1))
                for e in range(2):
                    send_b[f, pl.ds(q * 512 + 2 * p + e, YA, stride=8), :] = result[:, e * LANES:(e + 1) * LANES]
                return 0

            lax.fori_loop(0, 4, last_y, 0)
            target = (4 * col + q) * 64
            copy = pltpu.make_async_copy(
                chunk(send_b.at[f], q * 512 + col * 64, 64), chunk(outs[f], target, 64), local_sem.at[10 + 4 * f + q]
            )
            copy.start()
            pending.append(copy.wait)
            for j in range(1, COLS):
                other = lax.rem(col + j, COLS)
                remote(
                    chunk(send_b.at[f], q * 512 + other * 64, 64), chunk(outs[f], target, 64),
                    sends.at[7 + f], recv_sem_b.at[f], (row, other),
                ).start()

    some = 4 * (COLS - 1) * 64
    for f in range(2):
        remote(chunk(send_b.at[f], 0, some), chunk(outs[f], 0, some), sends.at[7 + f], recv_sem_b.at[f], neighbour).wait()
    remote(chunk(density, 0, some), chunk(buf, 0, some), sends.at[0], recv_sem_rows.at[0], neighbour).wait_send()
    for wait in pending:
        wait()


def on_device(counts, inverse_capacity):
    flat = (BINS // 4, LANES)
    vmem = pl.BlockSpec(memory_space=pltpu.VMEM)
    hbm = pl.BlockSpec(memory_space=pltpu.HBM)
    first, second = pl.pallas_call(
        kernel,
        out_shape=[jax.ShapeDtypeStruct(flat, F32)] * 2,
        in_specs=[hbm] * 4,
        out_specs=[vmem] * 2,
        scratch_shapes=[
            pltpu.VMEM(counts.shape, jnp.int32),
            pltpu.VMEM(counts.shape, F32),
            pltpu.VMEM(PRODUCTS.shape, F32),
            pltpu.VMEM(SINGLES.shape, F32),
            pltpu.VMEM(PRODUCTS.shape, BF16),
            pltpu.VMEM(PRODUCTS.shape, BF16),
            pltpu.VMEM((2 * YA, 3 * YA), BF16),
            pltpu.VMEM(flat, F32),
            pltpu.VMEM(flat, F32),
            pltpu.VMEM(flat, F32),
            pltpu.VMEM(flat, F32),
            pltpu.VMEM((4 * LANES, LANES), F32),
            pltpu.VMEM((2, DEVICES, 4, LANES), F32),
            pltpu.VMEM((2, DEVICES, 4, LANES), F32),
            pltpu.VMEM((1024, LANES), F32),
            pltpu.VMEM((8, 2 * LANES), F32),
            pltpu.VMEM((2, 8, 2 * LANES), F32),
            pltpu.VMEM((2, 2, DEVICES, 4, LANES), F32),
            pltpu.VMEM((2, 2, DEVICES, 4, LANES), F32),
            pltpu.VMEM((2,) + flat, F32),
            pltpu.SemaphoreType.DMA((4,)),
            pltpu.SemaphoreType.DMA((18,)),
            pltpu.SemaphoreType.DMA((9,)),
            pltpu.SemaphoreType.DMA((4,)),
            pltpu.SemaphoreType.DMA((2,)),
            pltpu.SemaphoreType.DMA((4,)),
            pltpu.SemaphoreType.DMA((2,)),
        ],
        compiler_params=pltpu.CompilerParams(
            collective_id=0, has_side_effects=True, vmem_limit_bytes=48 * 2**20
        ),
        name="field",
    )(*[
        pltpu.with_memory_space_constraint(x, pltpu.HBM)
        for x in (counts, inverse_capacity, jnp.asarray(PRODUCTS), jnp.asarray(SINGLES))
    ])

    def blocked(x):
        return x.reshape(32, 8, 8, LANES).transpose(0, 2, 1, 3).reshape(256, 1024)

    return blocked(first), blocked(second)


def solution(mesh):
    return jax.shard_map(
        on_device,
        mesh=mesh,
        in_specs=(P("row", "col"), P("row", "col")),
        out_specs=(P("row", "col"), P("row", "col")),
        check_vma=False,
    )
```

```python
import math

import jax
import jax.numpy as jnp
import numpy as np
from jax import lax
from jax.experimental import pallas as pl
from jax.experimental.pallas import tpu as pltpu
from jax.sharding import PartitionSpec as P

MESH = pl.DeviceIdType.MESH
F32 = jnp.float32
BF16 = jnp.bfloat16
ROWS, COLS = 32, 8
DEVICES = ROWS * COLS
LANES = 128
YA, YB = 64, 128
XA, XB = 256, 32
BINS = 8192


def tables(coarse, fine):
    half = fine // 2
    k = np.arange(coarse)[:, None]
    a = np.arange(coarse)[None, :]
    angle = np.pi * (k * a % (2 * coarse)) / coarse
    first = np.concatenate([np.cos(angle), np.sin(angle)], axis=0)
    first[coarse] = 1.0 - 2.0 * (np.arange(coarse) % 2)
    odd = 2 * np.arange(fine)[None, :] + 1
    turn = np.pi * k * odd / (2 * coarse * fine)
    m = np.arange(half)[:, None]
    low = np.pi * (m * odd % (2 * fine)) / fine
    high = np.pi * ((m + 1) * odd % (2 * fine)) / fine
    middle = np.pi * ((2 * m + 1) * odd % (4 * fine)) / (2 * fine)
    zero = np.zeros_like(low)
    cosine = np.block([[np.cos(low), -np.sin(low)], [np.cos(high), np.sin(high)]])
    cosine_top = np.block([[np.cos(low), zero], [zero, np.cos(middle)]])
    sine = np.block([[np.sin(low), np.cos(low)], [np.sin(high), -np.cos(high)]])
    sine_top = np.block([[np.sin(low), zero], [zero, np.sin(middle)]])
    place = np.arange(fine)[None, :]
    index = np.where(place < half, k + 2 * coarse * place, 2 * coarse * (place - half + 1) - k)
    index[0] = np.where(place[0] < half, 2 * coarse * place[0], coarse + 2 * coarse * (place[0] - half))
    return first, turn, cosine, cosine_top, sine, sine_top, index


def spread(matrix, copies):
    size = matrix.shape[0]
    left = np.kron(np.eye(copies), matrix[:, :size])
    right = np.kron(np.eye(copies), matrix[:, size:])
    return np.concatenate([left, right], axis=1)


def constants():
    products, singles = [], []
    first, turn, cosine, cosine_top, sine, sine_top, _ = tables(YA, YB)
    products += [("y_first", np.concatenate([first, np.zeros_like(first)], axis=1)), ("y_first_t", first.T)]
    singles += [("y_cos", np.cos(turn)), ("y_sin", np.sin(turn))]

    def seconds(axis, cosine, cosine_top, sine, sine_top):
        found = [(axis + "_second", cosine.T), (axis + "_second_top", cosine_top.T)]
        for name, table in (("_cos", cosine), ("_cos_top", cosine_top), ("_sin", sine), ("_sin_top", sine_top)):
            found += [(axis + name, table)]
        return found

    products += seconds("y", cosine, cosine_top, sine, sine_top)
    first, turn, cosine, cosine_top, sine, sine_top, index = tables(XA, XB)
    copies = LANES // XB
    products += [("x_first", first), ("x_first_t", first.T)]
    singles += [(name, np.tile(t, (1, copies))) for name, t in
                (("x_cos", np.cos(turn)), ("x_sin", np.sin(turn)), ("x_index", index))]
    products += seconds("x", *(spread(t, copies) for t in (cosine, cosine_top, sine, sine_top)))

    def pack(named):
        at, places = 0, {}
        for name, table in named:
            places[name] = (at, table.shape)
            at += table.size // LANES
        tiled = [
            table[:, lane:lane + LANES] for _, table in named for lane in range(0, table.shape[1], LANES)
        ]
        return np.concatenate(tiled, axis=0).astype(np.float32), places

    return pack(products) + pack(singles)


PRODUCTS, PRODUCT_AT, SINGLES, SINGLE_AT = constants()


def split(x):
    high = x.astype(BF16)
    return high, (x - high.astype(F32)).astype(BF16)


def dot(x, y):
    return jnp.dot(x, y, preferred_element_type=F32)


def times_table(x, table):
    high, low = split(x)
    t_high, t_low = table()
    return dot(high, t_high) + dot(low, t_high) + dot(high, t_low)


def table_times(table, x):
    high, low = split(x)
    t_high, t_low = table()
    return dot(t_high, high) + dot(t_high, low) + dot(t_low, high)


def kernel(
    counts_hbm, inverse_hbm, products_hbm, singles_hbm, out_first, out_second,
    counts, inverse, products, singles, table_high, table_low, y_stack, density, buf, bc, bs, turned, send_x, recv_x, spec, spec_top, sum_top,
    send_y, recv_y, send_b, load_sem, local_sem, sends, recv_sem_rows, recv_sem_x, recv_sem_y, recv_sem_b,
):
    def single(name):
        at, (height, _) = SINGLE_AT[name]
        return singles[at:at + height, :]

    def table(name):
        at, (height, width) = PRODUCT_AT[name]
        return lambda: [
            jnp.concatenate([part[at + t * height:at + (t + 1) * height, :] for t in range(width // LANES)], axis=1)
            for part in (table_high, table_low)
        ]

    outs = [out_first, out_second]
    pending = []
    loads = [
        pltpu.make_async_copy(counts_hbm, counts, load_sem.at[0]),
        pltpu.make_async_copy(inverse_hbm, inverse, load_sem.at[1]),
        pltpu.make_async_copy(products_hbm, products, load_sem.at[2]),
        pltpu.make_async_copy(singles_hbm, singles, load_sem.at[3]),
    ]
    for copy in loads:
        copy.start()

    row = lax.axis_index("row")
    col = lax.axis_index("col")
    me = row * COLS + col

    def place(device):
        return (device // COLS, device % COLS)

    def remote(src, dst, send, recv, device):
        return pltpu.make_async_remote_copy(
            src_ref=src, dst_ref=dst, send_sem=send, recv_sem=recv, device_id=device, device_id_type=MESH
        )

    barrier = pltpu.get_barrier_semaphore()

    for j in range(1, COLS):
        pl.semaphore_signal(barrier, inc=1, device_id=(row, lax.rem(col + j, COLS)), device_id_type=MESH)

    def greet(j, _):
        pl.semaphore_signal(barrier, inc=1, device_id=(lax.rem(row + j, ROWS), col), device_id_type=MESH)
        return 0

    lax.fori_loop(1, ROWS, greet, 0)

    loads[0].wait()
    loads[1].wait()

    def chunk(ref, at, size):
        return ref.at[pl.ds(pl.multiple_of(at, 8), size), :]

    own = []
    for q in range(4):

        def make_density(owner, _):
            at = pl.multiple_of(owner * 32 + q * 8, 8)
            values = counts[pl.ds(at, 8), :].astype(F32) * inverse[pl.ds(at, 8), :] * 0.03125
            for tile in range(8):
                to = pl.multiple_of(owner * 256 + q * 64 + tile * 8, 8)
                density[pl.ds(to, 8), :] = values[:, tile * LANES:(tile + 1) * LANES]
            return 0

        lax.fori_loop(0, 8, make_density, 0)
        if q == 0:
            pl.semaphore_wait(barrier, ROWS + COLS - 2)

        copy = pltpu.make_async_copy(
            chunk(density, col * 256 + q * 64, 64), chunk(buf, q * 512 + col * 64, 64), local_sem.at[q]
        )
        copy.start()
        own.append(copy)
        for j in range(1, COLS):
            other = lax.rem(col + j, COLS)
            remote(
                chunk(density, other * 256 + q * 64, 64), chunk(buf, q * 512 + col * 64, 64),
                sends.at[0], recv_sem_rows.at[q], (row, other),
            ).start()

    neighbour = (row, lax.rem(col + 1, COLS))

    loads[2].wait()
    loads[3].wait()

    def split_tables(t, _):
        at = pl.ds(pl.multiple_of(t * 64, 64), 64)
        table_high[at, :], table_low[at, :] = split(products[at, :])
        return 0

    lax.fori_loop(0, PRODUCTS.shape[0] // 64, split_tables, 0)
    high, low = (part[:, :YA] for part in table("y_first")())
    y_stack[...] = jnp.concatenate([high, high, low], axis=1)
    for q in range(4):
        own[q].wait()
        whole = chunk(buf, 0, (COLS - 1) * 64)
        remote(whole, whole, sends.at[0], recv_sem_rows.at[q], neighbour).wait_recv()

        def first_y(p, _):
            at = q * 512 + 2 * p
            pair = jnp.concatenate(
                [buf[pl.ds(at, YA, stride=8), :], buf[pl.ds(at + 1, YA, stride=8), :]], axis=1
            )
            high, low = split(pair)
            result = dot(y_stack[...], jnp.concatenate([high, low, high], axis=0))
            for e in range(2):
                i = q * 8 + 2 * p + e
                ac = result[:YA, e * LANES:(e + 1) * LANES]
                as_ = result[YA:, e * LANES:(e + 1) * LANES]
                bc[pl.ds(i, YA, stride=32), :] = ac * single("y_cos") - as_ * single("y_sin")
                bs[pl.ds(i, YA, stride=32), :] = ac * single("y_sin") + as_ * single("y_cos")
            return 0

        lax.fori_loop(0, 4, first_y, 0, unroll=True)

    def send_piece(src, dst, send, recv, other):
        remote(src.at[other], dst.at[me], send, recv, place(other)).start()

    def settle(src, dst, send, recv, local):
        copy = pltpu.make_async_copy(src.at[me], dst.at[me], local)
        copy.start()
        rest = remote(src.at[pl.ds(0, DEVICES - 1)], dst.at[pl.ds(0, DEVICES - 1)], send, recv, neighbour)
        pending.append(rest.wait_send)

        def arrived():
            copy.wait()
            rest.wait_recv()

        return arrived

    def exchange(src, dst, send, recv, local):
        def step(j, _):
            for e in range(5):
                send_piece(src, dst, send, recv, lax.rem(me + 1 + 5 * j + e, DEVICES))
            return 0

        lax.fori_loop(0, (DEVICES - 1) // 5, step, 0)
        return settle(src, dst, send, recv, local)

    channel = [
        (send_x.at[h], recv_x.at[h], sends.at[1 + h], recv_sem_x.at[h], local_sem.at[4 + h]) for h in range(2)
    ]

    def second_y(t, _):
        first = lax.rem(me // 64 + t, 4)
        at = pl.multiple_of(first * 512, 512)
        both = jnp.concatenate([bc[pl.ds(at, 512), :], bs[pl.ds(at, 512), :]], axis=1)
        turned[...] = times_table(both, table("y_second"))

        @pl.when(first == 0)
        def _():
            turned[:32, :] = times_table(both[:32], table("y_second_top"))

        for g in range(4):
            block = turned[g * LANES:(g + 1) * LANES, :].T
            for h in range(2):
                to = pl.multiple_of(first * 256 + g * 64, 64)
                send_x.at[h].reshape(1024, LANES)[pl.ds(to, 64), :] = block[h * 64:(h + 1) * 64]

        def step(other, _):
            send_piece(*channel[0][:4], other)
            return 0

        lax.fori_loop(jnp.where(t == 0, me + 1, first * 64), first * 64 + 64, step, 0)
        return 0

    lax.fori_loop(0, 4, second_y, 0)

    def rest_of_own(other, _):
        send_piece(*channel[0][:4], other)
        return 0

    lax.fori_loop(me // 64 * 64, me, rest_of_own, 0)
    arrived_x = [settle(*channel[0]), exchange(*channel[1])]
    spec_top[...] = jnp.zeros_like(spec_top)
    row_of = lax.broadcasted_iota(jnp.int32, (8, 2 * LANES), 0)
    norming = 4.0 / math.sqrt(BINS * BINS) / math.pi

    def v_of(half, step, shape):
        k = 4 * (me // 16) + lax.broadcasted_iota(jnp.int32, shape, 1) // XB
        m = 4 * lax.rem(me, 16) + step
        if half == 0:
            return (k + 2 * YA * m).astype(F32)
        return jnp.where(k == 0, 2 * YA * m + YA, 2 * YA * (m + 1) - k).astype(F32)

    arrived_y = {}
    for h in range(2):
        arrived_x[h]()
        pieces = recv_x.at[h].reshape(1024, LANES)

        def first_x(p, _):
            pair = jnp.concatenate(
                [pieces[pl.ds(2 * p, XA, stride=4), :], pieces[pl.ds(2 * p + 1, XA, stride=4), :]], axis=1
            )
            result = table_times(table("x_first"), pair)
            for e in range(2):
                s = 2 * p + e
                ac = result[:XA, e * LANES:(e + 1) * LANES]
                as_ = result[XA:, e * LANES:(e + 1) * LANES]
                both = jnp.concatenate(
                    [ac * single("x_cos") - as_ * single("x_sin"), ac * single("x_sin") + as_ * single("x_cos")],
                    axis=1,
                )
                spec[pl.ds(pl.multiple_of(s * XA, XA), XA), :] = times_table(both, table("x_second"))
                spec_top[pl.ds(s, 1), :] = both[:1]
            return 0

        lax.fori_loop(0, 2, first_x, 0, unroll=True)
        spec[pl.ds(0, 4, stride=XA), :] = times_table(spec_top[...], table("x_second_top"))[:4]

        def weigh(s, _):
            at = pl.multiple_of(s * XA, XA)
            v_row = v_of(h, s, (1, LANES))
            u = single("x_index")
            square = u * u + v_row * v_row
            corner = square == 0.0
            weight = jnp.where(corner, 0.0, norming / jnp.where(corner, 1.0, square))
            spec[pl.ds(at, XA), :] = spec[pl.ds(at, XA), :] * weight
            return 0

        lax.fori_loop(0, 4, weigh, 0, unroll=True)
        top = spec[pl.ds(0, 4, stride=XA), :]
        top = jnp.concatenate([top, jnp.zeros_like(top)], axis=0)
        tops = [
            times_table(top * single("x_index")[:1], table("x_sin_top")),
            times_table(top * v_of(h, lax.broadcasted_iota(jnp.int32, (8, LANES), 0), (8, LANES)), table("x_cos_top")),
        ]
        for f in range(2):
            sum_top[f] = tops[f]

        for f in range(2):
            target = send_y.at[f, h].reshape(1024, LANES)

            def sum_x(p, _):
                both = []
                for e in range(2):
                    s = 2 * p + e
                    value = spec[pl.ds(pl.multiple_of(s * XA, XA), XA), :]
                    factor = single("x_index") if f == 0 else v_of(h, s, (1, LANES))
                    result = times_table(value * factor, table(("x_sin", "x_cos")[f]))
                    head = jnp.sum(jnp.where(row_of == s, sum_top[f], 0.0), axis=0, keepdims=True)
                    head = jnp.where(row_of == 0, head, result[:8])
                    result = jnp.concatenate([head, result[8:]], axis=0)
                    gc, gs = result[:, :LANES], result[:, LANES:]
                    both.append(
                        jnp.concatenate(
                            [gc * single("x_cos") + gs * single("x_sin"), gs * single("x_cos") - gc * single("x_sin")],
                            axis=0,
                        )
                    )
                result = table_times(table("x_first_t"), jnp.concatenate(both, axis=1))
                for e in range(2):
                    target[pl.ds(2 * p + e, XA, stride=4), :] = result[:, e * LANES:(e + 1) * LANES]
                return 0

            lax.fori_loop(0, 2, sum_x, 0, unroll=True)
            arrived_y[f, h] = exchange(
                send_y.at[f, h], recv_y.at[f, h], sends.at[3 + 2 * f + h], recv_sem_y.at[2 * f + h],
                local_sem.at[6 + 2 * f + h],
            )

    for f in range(2):
        for h in range(2):
            arrived_y[f, h]()

        def sum_y(g, _):
            at = pl.multiple_of(g * LANES, LANES)
            half = pl.ds(pl.multiple_of(g * 64, 64), 64)
            value = jnp.concatenate([recv_y.at[f, h].reshape(1024, LANES)[half, :] for h in range(2)], axis=0).T
            result = times_table(value, table(("y_cos", "y_sin")[f]))
            bc[pl.ds(at, LANES), :] = result[:, :LANES]
            bs[pl.ds(at, LANES), :] = result[:, LANES:]

            @pl.when(g == 0)
            def _():
                result = times_table(value[:32], table(("y_cos_top", "y_sin_top")[f]))
                bc[:32, :] = result[:, :LANES]
                bs[:32, :] = result[:, LANES:]

            return 0

        lax.fori_loop(0, 16, sum_y, 0)
        for q in range(4):

            def last_y(p, _):
                both = []
                for e in range(2):
                    i = q * 8 + 2 * p + e
                    gc = bc[pl.ds(i, YA, stride=32), :]
                    gs = bs[pl.ds(i, YA, stride=32), :]
                    both.append(
                        jnp.concatenate(
                            [gc * single("y_cos") + gs * single("y_sin"), gs * single("y_cos") - gc * single("y_sin")], axis=0
                        )
                    )
                result = table_times(table("y_first_t"), jnp.concatenate(both, axis=1))
                for e in range(2):
                    send_b[f, pl.ds(q * 512 + 2 * p + e, YA, stride=8), :] = result[:, e * LANES:(e + 1) * LANES]
                return 0

            lax.fori_loop(0, 4, last_y, 0, unroll=True)
            target = (4 * col + q) * 64
            copy = pltpu.make_async_copy(
                chunk(send_b.at[f], q * 512 + col * 64, 64), chunk(outs[f], target, 64), local_sem.at[10 + 4 * f + q]
            )
            copy.start()
            pending.append(copy.wait)
            for j in range(1, COLS):
                other = lax.rem(col + j, COLS)
                remote(
                    chunk(send_b.at[f], q * 512 + other * 64, 64), chunk(outs[f], target, 64),
                    sends.at[7 + f], recv_sem_b.at[f], (row, other),
                ).start()

    some = 4 * (COLS - 1) * 64
    for f in range(2):
        remote(chunk(send_b.at[f], 0, some), chunk(outs[f], 0, some), sends.at[7 + f], recv_sem_b.at[f], neighbour).wait()
    remote(chunk(density, 0, some), chunk(buf, 0, some), sends.at[0], recv_sem_rows.at[0], neighbour).wait_send()
    for wait in pending:
        wait()


def settle_kernel(a, b, to_a, to_b, sem):
    copies = [pltpu.make_async_copy(a, to_a, sem.at[0]), pltpu.make_async_copy(b, to_b, sem.at[1])]
    for copy in copies:
        copy.start()
    for copy in copies:
        copy.wait()


def on_device(counts, inverse_capacity):
    flat = (BINS // 4, LANES)
    vmem = pl.BlockSpec(memory_space=pltpu.VMEM)
    hbm = pl.BlockSpec(memory_space=pltpu.HBM)
    first, second = pl.pallas_call(
        kernel,
        out_shape=[jax.ShapeDtypeStruct(flat, F32)] * 2,
        in_specs=[hbm] * 4,
        out_specs=[vmem] * 2,
        scratch_shapes=[
            pltpu.VMEM(counts.shape, jnp.int32),
            pltpu.VMEM(counts.shape, F32),
            pltpu.VMEM(PRODUCTS.shape, F32),
            pltpu.VMEM(SINGLES.shape, F32),
            pltpu.VMEM(PRODUCTS.shape, BF16),
            pltpu.VMEM(PRODUCTS.shape, BF16),
            pltpu.VMEM((2 * YA, 3 * YA), BF16),
            pltpu.VMEM(flat, F32),
            pltpu.VMEM(flat, F32),
            pltpu.VMEM(flat, F32),
            pltpu.VMEM(flat, F32),
            pltpu.VMEM((4 * LANES, LANES), F32),
            pltpu.VMEM((2, DEVICES, 4, LANES), F32),
            pltpu.VMEM((2, DEVICES, 4, LANES), F32),
            pltpu.VMEM((1024, LANES), F32),
            pltpu.VMEM((8, 2 * LANES), F32),
            pltpu.VMEM((2, 8, 2 * LANES), F32),
            pltpu.VMEM((2, 2, DEVICES, 4, LANES), F32),
            pltpu.VMEM((2, 2, DEVICES, 4, LANES), F32),
            pltpu.VMEM((2,) + flat, F32),
            pltpu.SemaphoreType.DMA((4,)),
            pltpu.SemaphoreType.DMA((18,)),
            pltpu.SemaphoreType.DMA((9,)),
            pltpu.SemaphoreType.DMA((4,)),
            pltpu.SemaphoreType.DMA((2,)),
            pltpu.SemaphoreType.DMA((4,)),
            pltpu.SemaphoreType.DMA((2,)),
        ],
        compiler_params=pltpu.CompilerParams(
            collective_id=0, has_side_effects=True, vmem_limit_bytes=48 * 2**20
        ),
        name="field",
    )(*[
        pltpu.with_memory_space_constraint(x, pltpu.HBM)
        for x in (counts, inverse_capacity, jnp.asarray(PRODUCTS), jnp.asarray(SINGLES))
    ])

    first, second = pl.pallas_call(
        settle_kernel,
        out_shape=[jax.ShapeDtypeStruct(flat, F32)] * 2,
        in_specs=[pl.BlockSpec(memory_space=pl.ANY)] * 2,
        out_specs=[hbm] * 2,
        scratch_shapes=[pltpu.SemaphoreType.DMA((2,))],
        compiler_params=pltpu.CompilerParams(vmem_limit_bytes=2**20),
        name="settle",
    )(first, second)

    def blocked(x):
        return x.reshape(32, 8, 8, LANES).transpose(0, 2, 1, 3).reshape(256, 1024)

    return blocked(first), blocked(second)


def solution(mesh):
    return jax.shard_map(
        on_device,
        mesh=mesh,
        in_specs=(P("row", "col"), P("row", "col")),
        out_specs=(P("row", "col"), P("row", "col")),
        check_vma=False,
    )
```

```python
import math

import jax
import jax.numpy as jnp
import numpy as np
from jax import lax
from jax.experimental import pallas as pl
from jax.experimental.pallas import tpu as pltpu
from jax.sharding import PartitionSpec as P

MESH = pl.DeviceIdType.MESH
F32 = jnp.float32
BF16 = jnp.bfloat16
ROWS, COLS = 32, 8
DEVICES = ROWS * COLS
LANES = 128
YA, YB = 64, 128
XA, XB = 256, 32
BINS = 8192


def tables(coarse, fine):
    half = fine // 2
    k = np.arange(coarse)[:, None]
    a = np.arange(coarse)[None, :]
    angle = np.pi * (k * a % (2 * coarse)) / coarse
    first = np.concatenate([np.cos(angle), np.sin(angle)], axis=0)
    first[coarse] = 1.0 - 2.0 * (np.arange(coarse) % 2)
    odd = 2 * np.arange(fine)[None, :] + 1
    turn = np.pi * k * odd / (2 * coarse * fine)
    m = np.arange(half)[:, None]
    low = np.pi * (m * odd % (2 * fine)) / fine
    high = np.pi * ((m + 1) * odd % (2 * fine)) / fine
    middle = np.pi * ((2 * m + 1) * odd % (4 * fine)) / (2 * fine)
    zero = np.zeros_like(low)
    cosine = np.block([[np.cos(low), -np.sin(low)], [np.cos(high), np.sin(high)]])
    cosine_top = np.block([[np.cos(low), zero], [zero, np.cos(middle)]])
    sine = np.block([[np.sin(low), np.cos(low)], [np.sin(high), -np.cos(high)]])
    sine_top = np.block([[np.sin(low), zero], [zero, np.sin(middle)]])
    place = np.arange(fine)[None, :]
    index = np.where(place < half, k + 2 * coarse * place, 2 * coarse * (place - half + 1) - k)
    index[0] = np.where(place[0] < half, 2 * coarse * place[0], coarse + 2 * coarse * (place[0] - half))
    return first, turn, cosine, cosine_top, sine, sine_top, index


def spread(matrix, copies):
    size = matrix.shape[0]
    left = np.kron(np.eye(copies), matrix[:, :size])
    right = np.kron(np.eye(copies), matrix[:, size:])
    return np.concatenate([left, right], axis=1)


def paired(table, field):
    out = np.zeros_like(table)
    for group in range(YB // 8):
        at = 8 * group + 4 * field
        out[at:at + 4] = table[4 * group:4 * group + 4]
    return out


def constants():
    products, singles = [], []
    first, turn, cosine, cosine_top, sine, sine_top, _ = tables(YA, YB)
    products += [("y_first", np.concatenate([first, np.zeros_like(first)], axis=1)), ("y_first_t", first.T)]
    singles += [("y_cos", np.cos(turn)), ("y_sin", np.sin(turn))]

    def seconds(axis, cosine, cosine_top, sine, sine_top):
        found = [(axis + "_second", cosine.T), (axis + "_second_top", cosine_top.T)]
        for name, table in (("_cos", cosine), ("_cos_top", cosine_top), ("_sin", sine), ("_sin_top", sine_top)):
            if axis == "x":
                found += [(axis + name, table)]
            else:
                found += [(axis + name, paired(table, int("sin" in name))), (axis + name + "_rest", table[YB // 2:])]
        return found

    products += seconds("y", cosine, cosine_top, sine, sine_top)
    first, turn, cosine, cosine_top, sine, sine_top, index = tables(XA, XB)
    copies = LANES // XB
    products += [("x_first", first), ("x_first_t", first.T)]
    singles += [(name, np.tile(t, (1, copies))) for name, t in
                (("x_cos", np.cos(turn)), ("x_sin", np.sin(turn)), ("x_index", index))]
    products += seconds("x", *(spread(t, copies) for t in (cosine, cosine_top, sine, sine_top)))

    def pack(named):
        at, places = 0, {}
        for name, table in named:
            places[name] = (at, table.shape)
            at += table.size // LANES
        tiled = [
            table[:, lane:lane + LANES] for _, table in named for lane in range(0, table.shape[1], LANES)
        ]
        return np.concatenate(tiled, axis=0).astype(np.float32), places

    return pack(products) + pack(singles)


PRODUCTS, PRODUCT_AT, SINGLES, SINGLE_AT = constants()


def split(x):
    high = x.astype(BF16)
    return high, (x - high.astype(F32)).astype(BF16)


def dot(x, y):
    return jnp.dot(x, y, preferred_element_type=F32)


def times_table(x, table):
    high, low = split(x)
    t_high, t_low = table()
    return dot(high, t_high) + dot(low, t_high) + dot(high, t_low)


def table_times(table, x):
    high, low = split(x)
    t_high, t_low = table()
    return dot(t_high, high) + dot(t_high, low) + dot(t_low, high)


def kernel(
    counts_hbm, inverse_hbm, products_hbm, singles_hbm, out_first, out_second,
    counts, inverse, products, singles, table_high, table_low, y_stack, density, buf, bc, bs, turned, send_x, recv_x, spec, spec_top, sum_top,
    send_pair, recv_pair, send_y, recv_y, send_b, load_sem, local_sem, sends, recv_sem_rows, recv_sem_x, recv_sem_y, recv_sem_b,
):
    def single(name):
        at, (height, _) = SINGLE_AT[name]
        return singles[at:at + height, :]

    def table(name):
        at, (height, width) = PRODUCT_AT[name]
        return lambda: [
            jnp.concatenate([part[at + t * height:at + (t + 1) * height, :] for t in range(width // LANES)], axis=1)
            for part in (table_high, table_low)
        ]

    outs = [out_first, out_second]
    pending = []
    loads = [
        pltpu.make_async_copy(counts_hbm, counts, load_sem.at[0]),
        pltpu.make_async_copy(inverse_hbm, inverse, load_sem.at[1]),
        pltpu.make_async_copy(products_hbm, products, load_sem.at[2]),
        pltpu.make_async_copy(singles_hbm, singles, load_sem.at[3]),
    ]
    for copy in loads:
        copy.start()

    row = lax.axis_index("row")
    col = lax.axis_index("col")
    me = row * COLS + col

    def place(device):
        return (device // COLS, device % COLS)

    def remote(src, dst, send, recv, device):
        return pltpu.make_async_remote_copy(
            src_ref=src, dst_ref=dst, send_sem=send, recv_sem=recv, device_id=device, device_id_type=MESH
        )

    barrier = pltpu.get_barrier_semaphore()

    for j in range(1, COLS):
        pl.semaphore_signal(barrier, inc=1, device_id=(row, lax.rem(col + j, COLS)), device_id_type=MESH)

    def greet(j, _):
        pl.semaphore_signal(barrier, inc=1, device_id=(lax.rem(row + j, ROWS), col), device_id_type=MESH)
        return 0

    lax.fori_loop(1, ROWS, greet, 0)

    loads[0].wait()
    loads[1].wait()

    def chunk(ref, at, size):
        return ref.at[pl.ds(pl.multiple_of(at, 8), size), :]

    own = []
    for q in range(4):

        def make_density(owner, _):
            at = pl.multiple_of(owner * 32 + q * 8, 8)
            values = counts[pl.ds(at, 8), :].astype(F32) * inverse[pl.ds(at, 8), :] * 0.03125
            for tile in range(8):
                to = pl.multiple_of(owner * 256 + q * 64 + tile * 8, 8)
                density[pl.ds(to, 8), :] = values[:, tile * LANES:(tile + 1) * LANES]
            return 0

        lax.fori_loop(0, 8, make_density, 0)
        if q == 0:
            pl.semaphore_wait(barrier, ROWS + COLS - 2)

        copy = pltpu.make_async_copy(
            chunk(density, col * 256 + q * 64, 64), chunk(buf, q * 512 + col * 64, 64), local_sem.at[q]
        )
        copy.start()
        own.append(copy)
        for j in range(1, COLS):
            other = lax.rem(col + j, COLS)
            remote(
                chunk(density, other * 256 + q * 64, 64), chunk(buf, q * 512 + col * 64, 64),
                sends.at[0], recv_sem_rows.at[q], (row, other),
            ).start()

    neighbour = (row, lax.rem(col + 1, COLS))

    loads[2].wait()
    loads[3].wait()

    def split_tables(t, _):
        at = pl.ds(pl.multiple_of(t * 64, 64), 64)
        table_high[at, :], table_low[at, :] = split(products[at, :])
        return 0

    lax.fori_loop(0, PRODUCTS.shape[0] // 64, split_tables, 0)
    high, low = (part[:, :YA] for part in table("y_first")())
    y_stack[...] = jnp.concatenate([high, high, low], axis=1)
    for q in range(4):
        own[q].wait()
        whole = chunk(buf, 0, (COLS - 1) * 64)
        remote(whole, whole, sends.at[0], recv_sem_rows.at[q], neighbour).wait_recv()

        def first_y(p, _):
            at = q * 512 + 2 * p
            pair = jnp.concatenate(
                [buf[pl.ds(at, YA, stride=8), :], buf[pl.ds(at + 1, YA, stride=8), :]], axis=1
            )
            high, low = split(pair)
            result = dot(y_stack[...], jnp.concatenate([high, low, high], axis=0))
            for e in range(2):
                i = q * 8 + 2 * p + e
                ac = result[:YA, e * LANES:(e + 1) * LANES]
                as_ = result[YA:, e * LANES:(e + 1) * LANES]
                bc[pl.ds(i, YA, stride=32), :] = ac * single("y_cos") - as_ * single("y_sin")
                bs[pl.ds(i, YA, stride=32), :] = ac * single("y_sin") + as_ * single("y_cos")
            return 0

        lax.fori_loop(0, 4, first_y, 0, unroll=True)

    def send_piece(src, dst, send, recv, other):
        remote(src.at[other], dst.at[me], send, recv, place(other)).start()

    def settle(src, dst, send, recv, local):
        copy = pltpu.make_async_copy(src.at[me], dst.at[me], local)
        copy.start()
        rest = remote(src.at[pl.ds(0, DEVICES - 1)], dst.at[pl.ds(0, DEVICES - 1)], send, recv, neighbour)
        pending.append(rest.wait_send)

        def arrived():
            copy.wait()
            rest.wait_recv()

        return arrived

    def exchange(src, dst, send, recv, local):
        def step(j, _):
            for e in range(5):
                send_piece(src, dst, send, recv, lax.rem(me + 1 + 5 * j + e, DEVICES))
            return 0

        lax.fori_loop(0, (DEVICES - 1) // 5, step, 0)
        return settle(src, dst, send, recv, local)

    channel = [
        (send_x.at[h], recv_x.at[h], sends.at[1 + h], recv_sem_x.at[h], local_sem.at[4 + h]) for h in range(2)
    ]

    def second_y(t, _):
        first = lax.rem(me // 64 + t, 4)
        at = pl.multiple_of(first * 512, 512)
        both = jnp.concatenate([bc[pl.ds(at, 512), :], bs[pl.ds(at, 512), :]], axis=1)
        turned[...] = times_table(both, table("y_second"))

        @pl.when(first == 0)
        def _():
            turned[:32, :] = times_table(both[:32], table("y_second_top"))

        for g in range(4):
            block = turned[g * LANES:(g + 1) * LANES, :].T
            for h in range(2):
                to = pl.multiple_of(first * 256 + g * 64, 64)
                send_x.at[h].reshape(1024, LANES)[pl.ds(to, 64), :] = block[h * 64:(h + 1) * 64]

        def step(other, _):
            send_piece(*channel[0][:4], other)
            return 0

        lax.fori_loop(jnp.where(t == 0, me + 1, first * 64), first * 64 + 64, step, 0)
        return 0

    lax.fori_loop(0, 4, second_y, 0)

    def rest_of_own(other, _):
        send_piece(*channel[0][:4], other)
        return 0

    lax.fori_loop(me // 64 * 64, me, rest_of_own, 0)
    arrived_x = [settle(*channel[0]), exchange(*channel[1])]
    spec_top[...] = jnp.zeros_like(spec_top)
    row_of = lax.broadcasted_iota(jnp.int32, (8, 2 * LANES), 0)
    norming = 4.0 / math.sqrt(BINS * BINS) / math.pi

    def v_of(half, step, shape):
        k = 4 * (me // 16) + lax.broadcasted_iota(jnp.int32, shape, 1) // XB
        m = 4 * lax.rem(me, 16) + step
        if half == 0:
            return (k + 2 * YA * m).astype(F32)
        return jnp.where(k == 0, 2 * YA * m + YA, 2 * YA * (m + 1) - k).astype(F32)

    arrived_y = {}
    for h in range(2):
        arrived_x[h]()
        pieces = recv_x.at[h].reshape(1024, LANES)

        def first_x(p, _):
            pair = jnp.concatenate(
                [pieces[pl.ds(2 * p, XA, stride=4), :], pieces[pl.ds(2 * p + 1, XA, stride=4), :]], axis=1
            )
            result = table_times(table("x_first"), pair)
            for e in range(2):
                s = 2 * p + e
                ac = result[:XA, e * LANES:(e + 1) * LANES]
                as_ = result[XA:, e * LANES:(e + 1) * LANES]
                both = jnp.concatenate(
                    [ac * single("x_cos") - as_ * single("x_sin"), ac * single("x_sin") + as_ * single("x_cos")],
                    axis=1,
                )
                spec[pl.ds(pl.multiple_of(s * XA, XA), XA), :] = times_table(both, table("x_second"))
                spec_top[pl.ds(s, 1), :] = both[:1]
            return 0

        lax.fori_loop(0, 2, first_x, 0, unroll=True)
        spec[pl.ds(0, 4, stride=XA), :] = times_table(spec_top[...], table("x_second_top"))[:4]

        def weigh(s, _):
            at = pl.multiple_of(s * XA, XA)
            v_row = v_of(h, s, (1, LANES))
            u = single("x_index")
            square = u * u + v_row * v_row
            corner = square == 0.0
            weight = jnp.where(corner, 0.0, norming / jnp.where(corner, 1.0, square))
            spec[pl.ds(at, XA), :] = spec[pl.ds(at, XA), :] * weight
            return 0

        lax.fori_loop(0, 4, weigh, 0, unroll=True)
        top = spec[pl.ds(0, 4, stride=XA), :]
        top = jnp.concatenate([top, jnp.zeros_like(top)], axis=0)
        tops = [
            times_table(top * single("x_index")[:1], table("x_sin_top")),
            times_table(top * v_of(h, lax.broadcasted_iota(jnp.int32, (8, LANES), 0), (8, LANES)), table("x_cos_top")),
        ]
        for f in range(2):
            sum_top[f] = tops[f]

        for f in range(2):
            target, size = (send_pair.reshape(2048, LANES), 8) if h == 0 else (send_y.at[f].reshape(1024, LANES), 4)
            start = 4 * f if h == 0 else 0

            def sum_x(p, _):
                both = []
                for e in range(2):
                    s = 2 * p + e
                    value = spec[pl.ds(pl.multiple_of(s * XA, XA), XA), :]
                    factor = single("x_index") if f == 0 else v_of(h, s, (1, LANES))
                    result = times_table(value * factor, table(("x_sin", "x_cos")[f]))
                    head = jnp.sum(jnp.where(row_of == s, sum_top[f], 0.0), axis=0, keepdims=True)
                    head = jnp.where(row_of == 0, head, result[:8])
                    result = jnp.concatenate([head, result[8:]], axis=0)
                    gc, gs = result[:, :LANES], result[:, LANES:]
                    both.append(
                        jnp.concatenate(
                            [gc * single("x_cos") + gs * single("x_sin"), gs * single("x_cos") - gc * single("x_sin")],
                            axis=0,
                        )
                    )
                result = table_times(table("x_first_t"), jnp.concatenate(both, axis=1))
                for e in range(2):
                    target[pl.ds(start + 2 * p + e, XA, stride=size), :] = result[:, e * LANES:(e + 1) * LANES]
                return 0

            lax.fori_loop(0, 2, sum_x, 0, unroll=True)
            if h == 1:
                arrived_y[f] = exchange(
                    send_y.at[f], recv_y.at[f], sends.at[4 + f], recv_sem_y.at[1 + f], local_sem.at[7 + f]
                )
        if h == 0:
            arrived_pair = exchange(send_pair, recv_pair, sends.at[3], recv_sem_y.at[0], local_sem.at[6])

    for f in range(2):
        if f == 0:
            arrived_pair()
        arrived_y[f]()
        name = ("y_cos", "y_sin")[f]

        def sum_y(g, _):
            at = pl.multiple_of(g * LANES, LANES)
            half = pl.ds(pl.multiple_of(g * 64, 64), 64)
            low = recv_pair.reshape(2048, LANES)[pl.ds(at, LANES), :].T
            high = recv_y.at[f].reshape(1024, LANES)[half, :].T
            result = times_table(low, table(name)) + times_table(high, table(name + "_rest"))
            bc[pl.ds(at, LANES), :] = result[:, :LANES]
            bs[pl.ds(at, LANES), :] = result[:, LANES:]

            @pl.when(g == 0)
            def _():
                top = times_table(low[:32], table(name + "_top"))
                top = top + times_table(high[:32], table(name + "_top_rest"))
                bc[:32, :] = top[:, :LANES]
                bs[:32, :] = top[:, LANES:]

            return 0

        lax.fori_loop(0, 16, sum_y, 0)
        for q in range(4):

            def last_y(p, _):
                both = []
                for e in range(2):
                    i = q * 8 + 2 * p + e
                    gc = bc[pl.ds(i, YA, stride=32), :]
                    gs = bs[pl.ds(i, YA, stride=32), :]
                    both.append(
                        jnp.concatenate(
                            [gc * single("y_cos") + gs * single("y_sin"), gs * single("y_cos") - gc * single("y_sin")], axis=0
                        )
                    )
                result = table_times(table("y_first_t"), jnp.concatenate(both, axis=1))
                for e in range(2):
                    send_b[f, pl.ds(q * 512 + 2 * p + e, YA, stride=8), :] = result[:, e * LANES:(e + 1) * LANES]
                return 0

            lax.fori_loop(0, 4, last_y, 0, unroll=True)
            target = (4 * col + q) * 64
            copy = pltpu.make_async_copy(
                chunk(send_b.at[f], q * 512 + col * 64, 64), chunk(outs[f], target, 64), local_sem.at[10 + 4 * f + q]
            )
            copy.start()
            pending.append(copy.wait)
            for j in range(1, COLS):
                other = lax.rem(col + j, COLS)
                remote(
                    chunk(send_b.at[f], q * 512 + other * 64, 64), chunk(outs[f], target, 64),
                    sends.at[7 + f], recv_sem_b.at[f], (row, other),
                ).start()

    some = 4 * (COLS - 1) * 64
    for f in range(2):
        remote(chunk(send_b.at[f], 0, some), chunk(outs[f], 0, some), sends.at[7 + f], recv_sem_b.at[f], neighbour).wait()
    remote(chunk(density, 0, some), chunk(buf, 0, some), sends.at[0], recv_sem_rows.at[0], neighbour).wait_send()
    for wait in pending:
        wait()


def settle_kernel(a, b, to_a, to_b, sem):
    copies = [pltpu.make_async_copy(a, to_a, sem.at[0]), pltpu.make_async_copy(b, to_b, sem.at[1])]
    for copy in copies:
        copy.start()
    for copy in copies:
        copy.wait()


def on_device(counts, inverse_capacity):
    flat = (BINS // 4, LANES)
    vmem = pl.BlockSpec(memory_space=pltpu.VMEM)
    hbm = pl.BlockSpec(memory_space=pltpu.HBM)
    first, second = pl.pallas_call(
        kernel,
        out_shape=[jax.ShapeDtypeStruct(flat, F32)] * 2,
        in_specs=[hbm] * 4,
        out_specs=[vmem] * 2,
        scratch_shapes=[
            pltpu.VMEM(counts.shape, jnp.int32),
            pltpu.VMEM(counts.shape, F32),
            pltpu.VMEM(PRODUCTS.shape, F32),
            pltpu.VMEM(SINGLES.shape, F32),
            pltpu.VMEM(PRODUCTS.shape, BF16),
            pltpu.VMEM(PRODUCTS.shape, BF16),
            pltpu.VMEM((2 * YA, 3 * YA), BF16),
            pltpu.VMEM(flat, F32),
            pltpu.VMEM(flat, F32),
            pltpu.VMEM(flat, F32),
            pltpu.VMEM(flat, F32),
            pltpu.VMEM((4 * LANES, LANES), F32),
            pltpu.VMEM((2, DEVICES, 4, LANES), F32),
            pltpu.VMEM((2, DEVICES, 4, LANES), F32),
            pltpu.VMEM((1024, LANES), F32),
            pltpu.VMEM((8, 2 * LANES), F32),
            pltpu.VMEM((2, 8, 2 * LANES), F32),
            pltpu.VMEM((DEVICES, 8, LANES), F32),
            pltpu.VMEM((DEVICES, 8, LANES), F32),
            pltpu.VMEM((2, DEVICES, 4, LANES), F32),
            pltpu.VMEM((2, DEVICES, 4, LANES), F32),
            pltpu.VMEM((2,) + flat, F32),
            pltpu.SemaphoreType.DMA((4,)),
            pltpu.SemaphoreType.DMA((18,)),
            pltpu.SemaphoreType.DMA((9,)),
            pltpu.SemaphoreType.DMA((4,)),
            pltpu.SemaphoreType.DMA((2,)),
            pltpu.SemaphoreType.DMA((4,)),
            pltpu.SemaphoreType.DMA((2,)),
        ],
        compiler_params=pltpu.CompilerParams(
            collective_id=0, has_side_effects=True, vmem_limit_bytes=48 * 2**20
        ),
        name="field",
    )(*[
        pltpu.with_memory_space_constraint(x, pltpu.HBM)
        for x in (counts, inverse_capacity, jnp.asarray(PRODUCTS), jnp.asarray(SINGLES))
    ])

    first, second = pl.pallas_call(
        settle_kernel,
        out_shape=[jax.ShapeDtypeStruct(flat, F32)] * 2,
        in_specs=[pl.BlockSpec(memory_space=pl.ANY)] * 2,
        out_specs=[hbm] * 2,
        scratch_shapes=[pltpu.SemaphoreType.DMA((2,))],
        compiler_params=pltpu.CompilerParams(vmem_limit_bytes=2**20),
        name="settle",
    )(first, second)

    def blocked(x):
        return x.reshape(32, 8, 8, LANES).transpose(0, 2, 1, 3).reshape(256, 1024)

    return blocked(first), blocked(second)


def solution(mesh):
    return jax.shard_map(
        on_device,
        mesh=mesh,
        in_specs=(P("row", "col"), P("row", "col")),
        out_specs=(P("row", "col"), P("row", "col")),
        check_vma=False,
    )
```
